32 devices in a mesh: tok: 4 (over x, core), voc: 8 (over z, y).
Axes of the slice: x: 2, y: 2, z: 4, core: 2. Of those that a mesh axis runs over, the one named last changes fastest.
Arguments:
- hidden: bfloat16 [64, 32, 2048], P(('tok', 'voc')), may hold values from -40 to 40
- norm_gain: float32 [2048], replicated, may hold values from 0.5 to 1.5
- head_weight: bfloat16 [2048, 51200], P(None, 'voc'), may hold values from -2 to 2
- lengths: int32 [64], P(('tok', 'voc')), may hold values from 12 to 24, as said below
- offsets: int32 [64], P(('tok', 'voc')), may hold values from 0 to 8
- slot_request: int32 [64], replicated, may hold values from 0 to 63, each once
- targets: int32 [64, 32], P(('tok', 'voc')), may hold values from 0 to 51199
Outputs:
- token_logprob: float32 [64, 32], P(('tok', 'voc'))
- token_entropy: float32 [64, 32], P(('tok', 'voc'))
The draws below stay inside these ranges and needn't reach their ends.
Inputs may be any that keep to these rules, and one draw needn't show every extreme that they name: `lengths`: each request has 12 to 24 response rows; all 2 requests of some one scoring device have exactly 24. Response rows end within the window: offsets + lengths <= 32. `slot_request`: every request appears in exactly one slot.
All inputs are finite; a program needn't handle non-finite values.
Results may differ from the reference program's by a relative error of at most 0.00145.
Values may be sent and summed in bfloat16 or wider, within the bound.
No kernel may reach another device: no remote copies, remote signals or barrier semaphores. Data moves between devices by JAX's collectives and lax.ppermute only.
A program may use at most 128 MiB of HBM per device.

```python
import jax
import jax.numpy as jnp
from jax import lax

D = 2048
SPAN = 32
LIVE = 24
REQ_DEV = 2
VOCAB = 51200
REQS = 64
N_VOC = 8


def special_columns(key):
    columns = jax.random.permutation(jax.random.fold_in(key, 31), VOCAB)[:6]
    vectors = jnp.clip(jax.random.normal(jax.random.fold_in(key, 32), (D, 3), jnp.float32), -3.0, 3.0)
    return (columns, vectors)


def draw_head_weight(key, part):
    weight = jnp.clip(jax.random.normal(jax.random.fold_in(key, 33), (D, VOCAB), jnp.float32), -5.0, 5.0) * (3.2 * D ** (-0.5))
    columns, vectors = special_columns(key)
    strength = jnp.array([2.5, 5.0, 7.5], jnp.float32)
    factor = 40.0 / D
    weight = weight.at[:, columns[:3]].set(vectors * strength[None, :] * factor)
    weight = weight.at[:, columns[3:]].set(vectors * (strength[None, :] - 0.05) * factor)
    return weight.astype(jnp.bfloat16)


def draw_hidden(key, part):
    values = jnp.clip(jax.random.normal(jax.random.fold_in(key, 21), (REQS, SPAN, D), jnp.float32), -6.0, 6.0)
    columns, vectors = special_columns(key)
    count = min(48, REQS * SPAN)
    planted_at = jax.random.permutation(jax.random.fold_in(key, 25), REQS * SPAN)[:count]
    which = jnp.arange(count) % 3
    noise = jax.random.normal(jax.random.fold_in(key, 26), (count, D), jnp.float32) * 0.01
    planted = vectors.T[which] + noise
    values = values.reshape(REQS * SPAN, D).at[planted_at].set(planted).reshape(REQS, SPAN, D)
    return values.astype(jnp.bfloat16)


def draw_lengths(key, part):
    drawn = jax.random.randint(jax.random.fold_in(key, 41), (REQS,), LIVE // 2, LIVE + 1)
    chosen = jax.random.randint(jax.random.fold_in(key, 42), (), 0, REQS // REQ_DEV)
    owners = jnp.arange(REQS, dtype=jnp.int32) // REQ_DEV
    return jnp.where(owners == chosen, LIVE, drawn).astype(jnp.int32)


def with_ends(entries, key, smallest, largest):
    place = [jax.random.randint(jax.random.fold_in(key, axis), (), 0, length) for axis, length in enumerate(entries.shape)]
    main_axis = entries.shape.index(max(entries.shape))
    beside = place[:main_axis] + [(place[main_axis] + 1) % entries.shape[main_axis]] + place[main_axis + 1:]
    return entries.at[tuple(place)].set(smallest).at[tuple(beside)].set(largest)


def setup_inputs(seed: int = 0) -> dict:
    keys = jax.random.split(jax.random.key(seed), 8)
    return {
        "hidden": draw_hidden(jax.random.fold_in(keys[7], 71), 0),
        "norm_gain": jnp.clip(1.0 + 0.1 * jax.random.normal(keys[1], (D,), jnp.float32), 0.5, 1.5),
        "head_weight": draw_head_weight(jax.random.fold_in(keys[7], 71), 0),
        "lengths": draw_lengths(jax.random.fold_in(keys[7], 71), 0),
        "offsets": with_ends(jax.random.randint(keys[4], (REQS,), 0, SPAN - LIVE + 1), jax.random.fold_in(keys[4], 1), 0, SPAN - LIVE).astype(jnp.int32),
        "slot_request": jax.random.permutation(keys[5], REQS).astype(jnp.int32),
        "targets": with_ends(jax.random.randint(keys[6], (REQS, SPAN), 0, VOCAB), jax.random.fold_in(keys[6], 1), 0, VOCAB - 1).astype(jnp.int32),
    }


EPS = 1e-06

def normalize(hidden, norm_gain):
    values = hidden.astype(jnp.float32)
    square = lax.optimization_barrier(jnp.mean(values * values, axis=-1, keepdims=True))
    return (values * lax.rsqrt(square + EPS) * norm_gain.astype(jnp.float32)).astype(jnp.bfloat16)

def reference(hidden, norm_gain, head_weight, lengths, offsets, slot_request, targets):
    normed = normalize(hidden, norm_gain)
    block = N_VOC * REQ_DEV * SPAN
    block_rows = normed.reshape(-1, block, D)
    block_goals = targets.reshape(-1, block)

    def one_block(item):
        rows_here, goals_here = item
        logits = jnp.dot(rows_here, head_weight, preferred_element_type=jnp.float32)
        row_peak = lax.optimization_barrier(jnp.max(logits, axis=1))
        scaled = jnp.exp(logits - row_peak[:, None])
        exp_sum = lax.optimization_barrier(jnp.sum(scaled, axis=1))
        exp_dot = lax.optimization_barrier(jnp.sum(scaled * logits, axis=1))
        picked = jnp.take_along_axis(logits, goals_here[:, None].astype(jnp.int32), axis=1)[:, 0]
        return (row_peak, exp_sum, exp_dot, picked)
    row_peak, exp_sum, exp_dot, picked = lax.map(one_block, (block_rows, block_goals))
    row_peak = row_peak.reshape(REQS, SPAN)
    exp_sum = exp_sum.reshape(REQS, SPAN)
    exp_dot = exp_dot.reshape(REQS, SPAN)
    picked = picked.reshape(REQS, SPAN)
    position = jnp.arange(SPAN, dtype=jnp.int32)[None, :]
    in_span = (position >= offsets[:, None]) & (position < offsets[:, None] + lengths[:, None])
    log_total = jnp.log(exp_sum)
    scored_logprob = jnp.where(in_span, picked - row_peak - log_total, 0.0)
    scored_entropy = jnp.where(in_span, row_peak + log_total - exp_dot / exp_sum, 0.0)
    token_logprob = jnp.zeros_like(scored_logprob).at[slot_request].set(scored_logprob)
    token_entropy = jnp.zeros_like(scored_entropy).at[slot_request].set(scored_entropy)
    return (token_logprob, token_entropy)
```

```python
import functools

import jax
import jax.numpy as jnp
from jax import lax
from jax.experimental import pallas as pl
from jax.experimental.pallas import tpu as pltpu
from jax.sharding import PartitionSpec as P

EPS = 1e-06
LIVE = 24
RING = 4
LANES = 128
DIGIT = 7
NOWHERE = (1 << (2 * DIGIT)) - 1
TILE = 1280
F32 = jnp.float32
BF16 = jnp.bfloat16
VMEM = pltpu.VMEM
MIB = 2**20


def iota(shape, dim):
    return lax.broadcasted_iota(jnp.int32, shape, dim)


def pack_kernel(n_voc, offset_ref, length_ref, request_ref, hidden_ref, gain_ref, target_ref, out_ref):
    req_dev, span, width = hidden_ref.shape
    rows = req_dev * LIVE
    device = lax.axis_index("tok") * n_voc + lax.axis_index("voc")
    values = hidden_ref[...].reshape(req_dev * span, width).astype(F32)
    square = jnp.mean(values * values, axis=-1, keepdims=True)
    normed = (values * lax.rsqrt(square + EPS) * gain_ref[...]).astype(BF16)
    row = iota((rows, 1), 0)
    source = jnp.zeros((rows, 1), jnp.int32)
    place = jnp.zeros((rows, 1), jnp.int32)
    target = jnp.zeros((rows, 1), F32)
    for slot in range(req_dev):
        step = row - slot * LIVE
        mine = (step >= 0) & (step < LIVE)
        position = offset_ref[slot] + step
        source = jnp.where(mine, slot * span + position, source)
        request = request_ref[device * req_dev + slot]
        scored = jnp.where(step < length_ref[slot], request * span + position, NOWHERE)
        place = jnp.where(mine, scored, place)
        found = mine & (iota((rows, span), 1) == position)
        ids = target_ref[slot : slot + 1, :].astype(F32)
        target += jnp.sum(jnp.where(found, ids, 0.0), axis=1, keepdims=True)
    taken = (iota((rows, req_dev * span), 1) == source).astype(BF16)
    out_ref[:, :width] = jnp.dot(taken, normed, preferred_element_type=F32).astype(BF16)
    target = target.astype(jnp.int32)
    low = (1 << DIGIT) - 1
    digits = (target >> (2 * DIGIT), (target >> DIGIT) & low, target & low, place >> DIGIT, place & low)
    lane = iota((rows, LANES), 1)
    tail = jnp.zeros((rows, LANES), jnp.int32)
    for at, digit in enumerate(digits):
        tail = jnp.where(lane == at, digit, tail)
    out_ref[:, width:] = tail.astype(F32).astype(BF16)


def pack(hidden, norm_gain, lengths, offsets, slot_request, targets, n_voc):
    req_dev, _, width = hidden.shape
    smem = pl.BlockSpec(memory_space=pltpu.SMEM)
    vmem = pl.BlockSpec(memory_space=VMEM)
    return pl.pallas_call(
        functools.partial(pack_kernel, n_voc),
        out_shape=jax.ShapeDtypeStruct((req_dev * LIVE, width + LANES), BF16),
        in_specs=[smem, smem, smem, vmem, vmem, vmem],
        out_specs=vmem,
        compiler_params=pltpu.CompilerParams(vmem_limit_bytes=8 * MIB),
        name="pack",
    )(offsets, lengths, slot_request, hidden, norm_gain.reshape(1, -1), targets)


def decode(tail):
    at, column = iota((LANES, 2 * LANES), 0), iota((LANES, 2 * LANES), 1)
    first = column < LANES
    scale = jnp.zeros((LANES, 2 * LANES), F32)
    for row, value in enumerate((1 << (2 * DIGIT), 1 << DIGIT, 1)):
        scale = jnp.where(first & (at == row), float(value), scale)
    for row, value in enumerate((1 << DIGIT, 1)):
        scale = jnp.where((~first) & (at == row + 3), float(value), scale)
    both = jnp.dot(tail, scale.astype(BF16), preferred_element_type=F32)
    return both[:, :LANES], both[:, LANES:]


def score_kernel(count, carried, per_dev, *refs):
    blocks, weight_ref = refs[:count], refs[count]
    before = refs[count + 1] if carried else None
    out_ref, x_ref, peak_ref, sum_ref, dot_ref, pick_ref, place_ref = refs[count + 1 + carried :]
    size = blocks[0].shape[0]
    rows, width = x_ref.shape
    vocab_dev = weight_ref.shape[1]
    lane = iota((rows, LANES), 1).astype(F32)
    for at, block in enumerate(blocks):
        x_ref[at * size : (at + 1) * size, :] = block[:, :width]
    tails = jnp.concatenate([block[:, width:] for block in blocks], axis=0)
    target, place = decode(tails)
    place_ref[...] = place
    first_column = (lax.axis_index("voc") * vocab_dev).astype(F32)
    wanted = target - lane - first_column
    peak_ref[...] = jnp.full((rows, LANES), -jnp.inf, F32)
    for ref in (sum_ref, dot_ref, pick_ref):
        ref[...] = jnp.zeros((rows, LANES), F32)

    def step(i, _):
        base = pl.multiple_of(i * TILE, TILE)
        logits = jnp.dot(x_ref[...], weight_ref[:, pl.ds(base, TILE)], preferred_element_type=F32)
        parts = [logits[:, at : at + LANES] for at in range(0, TILE, LANES)]
        old = peak_ref[...]
        peak = functools.reduce(jnp.maximum, parts, old)
        drop = jnp.where(i > 0, old - peak, 0.0)
        scale = jnp.exp(drop)
        total = sum_ref[...]
        dots = (dot_ref[...] + drop * total) * scale
        total = total * scale
        pick = pick_ref[...]
        for at, part in enumerate(parts):
            below = part - peak
            weight = jnp.exp(below)
            total += weight
            dots += weight * below
            pick = jnp.where(wanted == (base + at * LANES).astype(F32), part, pick)
        peak_ref[...] = peak
        sum_ref[...] = total
        dot_ref[...] = dots
        pick_ref[...] = pick
        return 0

    lax.fori_loop(0, vocab_dev // TILE, step, 0)
    peak = jnp.max(peak_ref[...], axis=1, keepdims=True)
    drop = peak_ref[...] - peak
    scale = jnp.exp(drop)
    total = jnp.sum(sum_ref[...] * scale, axis=1, keepdims=True)
    dots = jnp.sum((dot_ref[...] + drop * sum_ref[...]) * scale, axis=1, keepdims=True)
    pick = jnp.sum(pick_ref[...], axis=1, keepdims=True)
    stats = jnp.zeros((rows, LANES), F32)
    for at, value in enumerate((peak, total, dots, pick)):
        high = value.astype(BF16).astype(F32)
        middle = (value - high).astype(BF16).astype(F32)
        low = value - high - middle
        for part, piece in enumerate((high, middle, low)):
            stats = jnp.where(lane == float(8 * part + at), piece, stats)
    stats = stats.T.astype(BF16)[:32]
    for group in range(out_ref.shape[0] * per_dev // LANES):
        there = (place_ref[...] == lane + float(group * LANES)).astype(F32).astype(BF16)
        moved = jnp.dot(stats, there, preferred_element_type=F32)
        moved = moved[0:8] + moved[8:16] + moved[16:24]
        for at in range(LANES // per_dev):
            to = group * (LANES // per_dev) + at
            part = moved[:, at * per_dev : (at + 1) * per_dev]
            if carried:
                part += before[to, :, :per_dev]
            out_ref[to, :, :per_dev] = part


def score(blocks, weight, before, n_dev, per_dev):
    count = len(blocks)
    size, wide = blocks[0].shape
    rows, width = count * size, wide - LANES
    operands = [pltpu.with_memory_space_constraint(a, VMEM) for a in (*blocks, weight)]
    if before is not None:
        operands.append(before)
    vmem = pl.BlockSpec(memory_space=VMEM)
    state = VMEM((rows, LANES), F32)
    vocab_dev = weight.shape[1]
    return pl.pallas_call(
        functools.partial(score_kernel, count, before is not None, per_dev),
        out_shape=jax.ShapeDtypeStruct((n_dev, 8, LANES), F32),
        in_specs=[vmem] * len(operands),
        out_specs=vmem,
        scratch_shapes=[VMEM((rows, width), BF16)] + [state] * 5,
        compiler_params=pltpu.CompilerParams(vmem_limit_bytes=16 * MIB),
        cost_estimate=pl.CostEstimate(
            flops=2 * rows * width * vocab_dev,
            bytes_accessed=2 * width * vocab_dev,
            transcendentals=rows * vocab_dev,
        ),
        name="score",
    )(*operands)


def finish_kernel(all_ref, logprob_ref, entropy_ref):
    req_dev, span = logprob_ref.shape
    peak, total, dots, pick = (all_ref[:, at, :] for at in range(4))
    held = total > 0.0
    top = jnp.max(jnp.where(held, peak, -jnp.inf), axis=0, keepdims=True)
    scored = top > -jnp.inf
    top = jnp.where(scored, top, 0.0)
    drop = jnp.where(held, peak - top, 0.0)
    scale = jnp.exp(drop)
    whole = jnp.sum(total * scale, axis=0, keepdims=True)
    whole = jnp.where(scored, whole, 1.0)
    mean = jnp.sum((dots + drop * total) * scale, axis=0, keepdims=True) / whole
    log_total = jnp.log(whole)
    logprob = jnp.where(scored, jnp.sum(pick, axis=0, keepdims=True) - top - log_total, 0.0)
    entropy = jnp.where(scored, log_total - mean, 0.0)
    for at in range(req_dev):
        logprob_ref[at : at + 1, :] = logprob[:, at * span : (at + 1) * span]
        entropy_ref[at : at + 1, :] = entropy[:, at * span : (at + 1) * span]


def finish(everything, req_dev, span):
    vmem = pl.BlockSpec(memory_space=VMEM)
    shape = jax.ShapeDtypeStruct((req_dev, span), F32)
    return pl.pallas_call(
        finish_kernel,
        out_shape=(shape, shape),
        in_specs=[vmem],
        out_specs=(vmem, vmem),
        compiler_params=pltpu.CompilerParams(vmem_limit_bytes=8 * MIB),
        name="finish",
    )(everything)


def shift(block, along_z, along_y, n_voc):
    side = n_voc // RING
    pairs = [
        (z * side + y, (z + along_z) % RING * side + (y + along_y) % side)
        for z in range(RING)
        for y in range(side)
    ]
    return lax.ppermute(block, "voc", pairs)


def shards(n_tok, n_voc, hidden, norm_gain, head_weight, lengths, offsets, slot_request, targets):
    req_dev, span, _ = hidden.shape
    n_dev = n_tok * n_voc
    own = pack(hidden, norm_gain, lengths, offsets, slot_request, targets, n_voc)
    side = n_voc // RING
    steps = [(z, y) for z in range(RING) for y in range(side)]
    steps.sort(key=lambda at: (min(at[0], RING - at[0]) + min(at[1], side - at[1]), at[0]))
    blocks = [own] + [shift(own, z, y, n_voc) for z, y in steps[1:]]
    half = len(blocks) // 2
    sent = score(blocks[:half], head_weight, None, n_dev, req_dev * span)
    sent = score(blocks[half:], head_weight, sent, n_dev, req_dev * span)
    everything = lax.all_to_all(sent, ("tok", "voc"), 0, 0, tiled=True)
    return finish(everything, req_dev, span)


def solution(mesh):
    placed = (
        P(("tok", "voc"), None, None),
        P(),
        P(None, "voc"),
        P(("tok", "voc")),
        P(("tok", "voc")),
        P(),
        P(("tok", "voc"), None),
    )
    return jax.shard_map(
        functools.partial(shards, mesh.shape["tok"], mesh.shape["voc"]),
        mesh=mesh,
        in_specs=placed,
        out_specs=(P(("tok", "voc"), None), P(("tok", "voc"), None)),
        check_vma=False,
    )
```

```python
import functools

import jax
import jax.numpy as jnp
from jax import lax
from jax.experimental import pallas as pl
from jax.experimental.pallas import tpu as pltpu
from jax.sharding import PartitionSpec as P

EPS = 1e-06
LIVE = 24
RING = 4
LANES = 128
DIGIT = 7
NOWHERE = (1 << (2 * DIGIT)) - 1
STATS = 4
TILE = 1280
PIECE = 512
AHEAD = 4
MOST = 4
F32 = jnp.float32
BF16 = jnp.bfloat16
VMEM = pltpu.VMEM
MIB = 2**20


def iota(shape, dim):
    return lax.broadcasted_iota(jnp.int32, shape, dim)


def pack_kernel(n_voc, *refs):
    sources, out_ref, copies, sems = refs[:6], refs[6], refs[7:13], refs[13]
    started = [pltpu.make_async_copy(a, b, sems.at[at]) for at, (a, b) in enumerate(zip(sources, copies))]
    for copy in started:
        copy.start()
    for copy in started:
        copy.wait()
    offset_ref, length_ref, request_ref, hidden_ref, gain_ref, target_ref = copies
    req_dev, span, width = hidden_ref.shape
    rows = req_dev * LIVE
    device = lax.axis_index("tok") * n_voc + lax.axis_index("voc")
    values = hidden_ref[...].reshape(req_dev * span, width).astype(F32)
    square = jnp.mean(values * values, axis=-1, keepdims=True)
    normed = (values * lax.rsqrt(square + EPS) * gain_ref[...]).astype(BF16)
    row = iota((rows, 1), 0)
    source = jnp.zeros((rows, 1), jnp.int32)
    place = jnp.zeros((rows, 1), jnp.int32)
    target = jnp.zeros((rows, 1), F32)
    for slot in range(req_dev):
        step = row - slot * LIVE
        mine = (step >= 0) & (step < LIVE)
        position = offset_ref[slot] + step
        source = jnp.where(mine, slot * span + position, source)
        request = request_ref[device * req_dev + slot]
        scored = jnp.where(step < length_ref[slot], request * span + position, NOWHERE)
        place = jnp.where(mine, scored, place)
        found = mine & (iota((rows, span), 1) == position)
        ids = target_ref[slot : slot + 1, :].astype(F32)
        target += jnp.sum(jnp.where(found, ids, 0.0), axis=1, keepdims=True)
    taken = (iota((rows, req_dev * span), 1) == source).astype(BF16)
    out_ref[:, :width] = jnp.dot(taken, normed, preferred_element_type=F32).astype(BF16)
    target = target.astype(jnp.int32)
    low = (1 << DIGIT) - 1
    digits = (target >> (2 * DIGIT), (target >> DIGIT) & low, target & low, place >> DIGIT, place & low)
    lane = iota((rows, LANES), 1)
    tail = jnp.zeros((rows, LANES), jnp.int32)
    for at, digit in enumerate(digits):
        tail = jnp.where(lane == at, digit, tail)
    out_ref[:, width:] = tail.astype(F32).astype(BF16)


def pack(hidden, norm_gain, lengths, offsets, slot_request, targets, n_voc):
    req_dev, _, width = hidden.shape
    arrays = (offsets, lengths, slot_request, hidden, norm_gain.reshape(1, -1), targets)
    spaces = (pltpu.SMEM,) * 3 + (VMEM,) * 3
    return pl.pallas_call(
        functools.partial(pack_kernel, n_voc),
        out_shape=jax.ShapeDtypeStruct((req_dev * LIVE, width + LANES), BF16),
        in_specs=[pl.BlockSpec(memory_space=pl.ANY)] * 6,
        out_specs=pl.BlockSpec(memory_space=VMEM),
        scratch_shapes=[space(a.shape, a.dtype) for space, a in zip(spaces, arrays)]
        + [pltpu.SemaphoreType.DMA((6,))],
        compiler_params=pltpu.CompilerParams(vmem_limit_bytes=8 * MIB),
        name="pack",
    )(*(pltpu.with_memory_space_constraint(a, pltpu.HBM) for a in arrays))


def decode(tail):
    at, column = iota((LANES, 2 * LANES), 0), iota((LANES, 2 * LANES), 1)
    first = column < LANES
    scale = jnp.zeros((LANES, 2 * LANES), F32)
    for row, value in enumerate((1 << (2 * DIGIT), 1 << DIGIT, 1)):
        scale = jnp.where(first & (at == row), float(value), scale)
    for row, value in enumerate((1 << DIGIT, 1)):
        scale = jnp.where((~first) & (at == row + 3), float(value), scale)
    both = jnp.dot(tail, scale.astype(BF16), preferred_element_type=F32)
    return both[:, :LANES], both[:, LANES:]


def tiles(columns, size):
    return [(base, min(size, columns - base)) for base in range(0, columns, size)]


def assemble(blocks, x_ref, place_ref):
    size, width = blocks[0].shape[0], x_ref.shape[1]
    for at, block in enumerate(blocks):
        x_ref[at * size : (at + 1) * size, :] = block[:, :width]
    target, place = decode(jnp.concatenate([block[:, width:] for block in blocks], axis=0))
    place_ref[...] = place
    return target


def take(logits_ref, state, wanted, base, wide, fresh):
    peak_ref, sum_ref, dot_ref, pick_ref = state
    peak = functools.reduce(jnp.maximum, [logits_ref[:, at : at + LANES] for at in range(0, wide, LANES)])
    if fresh:
        total = dots = pick = jnp.zeros_like(peak)
    else:
        old = peak_ref[...]
        peak = jnp.maximum(old, peak)
        drop = old - peak
        scale = jnp.exp(drop)
        total = sum_ref[...]
        dots = (dot_ref[...] + drop * total) * scale
        total = total * scale
        pick = pick_ref[...]
    for at in range(0, wide, LANES):
        part = logits_ref[:, at : at + LANES]
        below = part - peak
        weight = jnp.exp(below)
        total += weight
        dots += weight * below
        pick = jnp.where(wanted == float(base + at), part, pick)
    peak_ref[...] = peak
    sum_ref[...] = total
    dot_ref[...] = dots
    pick_ref[...] = pick


def route(state, place_ref, before_ref, out_ref, per_dev):
    peak_ref, sum_ref, dot_ref, pick_ref = state
    rows = place_ref.shape[0]
    lane = iota((rows, LANES), 1).astype(F32)
    peak = jnp.max(peak_ref[...], axis=1, keepdims=True)
    drop = peak_ref[...] - peak
    scale = jnp.exp(drop)
    total = jnp.sum(sum_ref[...] * scale, axis=1, keepdims=True)
    dots = jnp.sum((dot_ref[...] + drop * sum_ref[...]) * scale, axis=1, keepdims=True)
    pick = jnp.sum(pick_ref[...], axis=1, keepdims=True)
    stats = jnp.zeros((rows, LANES), F32)
    for at, value in enumerate((peak, total, dots, pick)):
        high = value.astype(BF16).astype(F32)
        middle = (value - high).astype(BF16).astype(F32)
        low = value - high - middle
        for part, piece in enumerate((high, middle, low)):
            stats = jnp.where(lane == float(8 * part + at), piece, stats)
    stats = stats.T.astype(BF16)[:32]
    for group in range(out_ref.shape[0] * per_dev // LANES):
        there = (place_ref[...] == lane + float(group * LANES)).astype(F32).astype(BF16)
        moved = jnp.dot(stats, there, preferred_element_type=F32)
        moved = (moved[0:8] + moved[8:16] + moved[16:24])[:STATS]
        for at in range(LANES // per_dev):
            to = group * (LANES // per_dev) + at
            part = moved[:, at * per_dev : (at + 1) * per_dev]
            if before_ref is not None:
                part += before_ref[to, :, :per_dev]
            out_ref[to, :, :per_dev] = part


def sweep(x_ref, plan, logits, state, wanted, fresh):
    last = None
    for at, (weight_ref, column, base, wide, wait) in enumerate(plan):
        wait()
        logits[at % 2][:, :wide] = jnp.dot(
            x_ref[...], weight_ref[:, column : column + wide], preferred_element_type=F32
        )
        if last is not None:
            take(logits[(at - 1) % 2], state, wanted, *last, fresh and at == 1)
        last = (base, wide)
    take(logits[(len(plan) - 1) % 2], state, wanted, *last, fresh and len(plan) == 1)


def wanted_columns(target, vocab_dev):
    first = (lax.axis_index("voc") * vocab_dev).astype(F32)
    return target - first - iota(target.shape, 1).astype(F32)


def load_kernel(count, lo, hi, per_dev, *refs):
    last = hi is None
    blocks, (weight_ref, *refs) = refs[:count], refs[count:]
    if last:
        before_ref, out_ref, held_ref, *refs = refs
    else:
        state_ref, held_ref, *refs = refs
    x_ref, place_ref, even_ref, odd_ref, sems, *refs = refs
    vocab_dev = weight_ref.shape[1]
    hi = vocab_dev if last else hi
    plan = tiles(hi - lo, PIECE)
    fetches = [
        pltpu.make_async_copy(
            weight_ref.at[:, pl.ds(lo + base, wide)], held_ref.at[:, pl.ds(base, wide)], sems.at[at]
        )
        for at, (base, wide) in enumerate(plan)
    ]
    for fetch in fetches[:AHEAD]:
        fetch.start()
    target = assemble(blocks, x_ref, place_ref)
    state = refs if last else [state_ref.at[at] for at in range(STATS)]
    if last:
        for at in range(STATS):
            state[at][...] = before_ref[at]

    def arrival(at):
        def wait():
            fetches[at].wait()
            if at + AHEAD < len(fetches):
                fetches[at + AHEAD].start()

        return wait

    steps = [(held_ref, base, lo + base, wide, arrival(at)) for at, (base, wide) in enumerate(plan)]
    sweep(x_ref, steps, (even_ref, odd_ref), state, wanted_columns(target, vocab_dev), not last)
    if last:
        route(state, place_ref, None, out_ref, per_dev)


def load(blocks, weight, before, lo, hi, n_dev, per_dev):
    rows, width = len(blocks) * blocks[0].shape[0], blocks[0].shape[1] - LANES
    vocab_dev = weight.shape[1]
    last = before is not None
    count = (vocab_dev if last else hi) - lo
    vmem = pl.BlockSpec(memory_space=VMEM)
    result = (n_dev, STATS, LANES) if last else (STATS, rows, LANES)
    operands = [pltpu.with_memory_space_constraint(a, VMEM) for a in blocks]
    operands.append(pltpu.with_memory_space_constraint(weight, pltpu.HBM))
    operands += [before] if last else []
    state = VMEM((rows, LANES), F32)
    return pl.pallas_call(
        functools.partial(load_kernel, len(blocks), lo, None if last else hi, per_dev),
        out_shape=(jax.ShapeDtypeStruct(result, F32), VMEM((width, count), BF16)),
        in_specs=[vmem] * len(blocks) + [pl.BlockSpec(memory_space=pl.ANY)] + [vmem] * last,
        out_specs=(vmem, vmem),
        scratch_shapes=[VMEM((rows, width), BF16), state]
        + [VMEM((rows, PIECE), F32)] * 2
        + [pltpu.SemaphoreType.DMA((len(tiles(count, PIECE)),))]
        + [state] * (STATS * last),
        compiler_params=pltpu.CompilerParams(vmem_limit_bytes=6 * MIB),
        cost_estimate=pl.CostEstimate(
            flops=2 * rows * width * count, bytes_accessed=2 * width * count, transcendentals=rows * count
        ),
        name="load",
    )(*operands)


def score_kernel(count, carried, per_dev, *refs):
    blocks, (first_ref, second_ref, *refs) = refs[:count], refs[count:]
    if carried:
        before_ref, *refs = refs
    out_ref, x_ref, place_ref, even_ref, odd_ref, *state = refs
    cut = first_ref.shape[1]
    target = assemble(blocks, x_ref, place_ref)
    steps = [(first_ref, base, base, wide, lambda: None) for base, wide in tiles(cut, TILE)]
    steps += [(second_ref, base, cut + base, wide, lambda: None) for base, wide in tiles(second_ref.shape[1], TILE)]
    wanted = wanted_columns(target, cut + second_ref.shape[1])
    sweep(x_ref, steps, (even_ref, odd_ref), state, wanted, True)
    route(state, place_ref, before_ref if carried else None, out_ref, per_dev)


def score(blocks, weights, before, n_dev, per_dev):
    count = len(blocks)
    rows, width = count * blocks[0].shape[0], blocks[0].shape[1] - LANES
    vocab_dev = sum(a.shape[1] for a in weights)
    vmem = pl.BlockSpec(memory_space=VMEM)
    operands = [pltpu.with_memory_space_constraint(a, VMEM) for a in (*blocks, *weights)]
    operands += [] if before is None else [before]
    state = VMEM((rows, LANES), F32)
    return pl.pallas_call(
        functools.partial(score_kernel, count, before is not None, per_dev),
        out_shape=jax.ShapeDtypeStruct((n_dev, STATS, LANES), F32),
        in_specs=[vmem] * len(operands),
        out_specs=vmem,
        scratch_shapes=[VMEM((rows, width), BF16), state] + [VMEM((rows, TILE), F32)] * 2 + [state] * STATS,
        compiler_params=pltpu.CompilerParams(vmem_limit_bytes=10 * MIB),
        cost_estimate=pl.CostEstimate(
            flops=2 * rows * width * vocab_dev,
            bytes_accessed=2 * width * vocab_dev,
            transcendentals=rows * vocab_dev,
        ),
        name="score",
    )(*operands)


def finish_kernel(all_ref, logprob_ref, entropy_ref):
    req_dev, span = logprob_ref.shape
    peak, total, dots, pick = (all_ref[:, at, :] for at in range(4))
    held = total > 0.0
    top = jnp.max(jnp.where(held, peak, -jnp.inf), axis=0, keepdims=True)
    scored = top > -jnp.inf
    top = jnp.where(scored, top, 0.0)
    drop = jnp.where(held, peak - top, 0.0)
    scale = jnp.exp(drop)
    whole = jnp.sum(total * scale, axis=0, keepdims=True)
    whole = jnp.where(scored, whole, 1.0)
    mean = jnp.sum((dots + drop * total) * scale, axis=0, keepdims=True) / whole
    log_total = jnp.log(whole)
    logprob = jnp.where(scored, jnp.sum(pick, axis=0, keepdims=True) - top - log_total, 0.0)
    entropy = jnp.where(scored, log_total - mean, 0.0)
    for at in range(req_dev):
        logprob_ref[at : at + 1, :] = logprob[:, at * span : (at + 1) * span]
        entropy_ref[at : at + 1, :] = entropy[:, at * span : (at + 1) * span]


def finish(everything, req_dev, span):
    vmem = pl.BlockSpec(memory_space=VMEM)
    shape = jax.ShapeDtypeStruct((req_dev, span), F32)
    return pl.pallas_call(
        finish_kernel,
        out_shape=(shape, shape),
        in_specs=[vmem],
        out_specs=(vmem, vmem),
        compiler_params=pltpu.CompilerParams(vmem_limit_bytes=8 * MIB),
        name="finish",
    )(everything)


def shift(block, along_z, along_y, n_voc):
    side = n_voc // RING
    pairs = [
        (z * side + y, (z + along_z) % RING * side + (y + along_y) % side)
        for z in range(RING)
        for y in range(side)
    ]
    return lax.ppermute(block, "voc", pairs)


def shards(n_tok, n_voc, hidden, norm_gain, head_weight, lengths, offsets, slot_request, targets):
    req_dev, span, _ = hidden.shape
    n_dev, per_dev = n_tok * n_voc, req_dev * span
    over_y = range(1, n_voc // RING)
    cut = (head_weight.shape[1] // 256 + 1) // 2 * 256
    own = pack(hidden, norm_gain, lengths, offsets, slot_request, targets, n_voc)
    below = shift(own, -1, 0, n_voc)
    beside = [shift(own, 0, y, n_voc) for y in over_y]
    above = shift(own, 1, 0, n_voc)
    sums, first = load([own], head_weight, None, 0, cut, n_dev, per_dev)
    sums, below, beside, above, own = lax.optimization_barrier((sums, below, beside, above, own))
    far = shift(below, -1, 0, n_voc)
    corners = [shift(a, 1, 0, n_voc) for a in beside] + [shift(below, 0, y, n_voc) for y in over_y]
    sent, second = load([own], head_weight, sums, cut, None, n_dev, per_dev)
    sent, far = lax.optimization_barrier((sent, far))
    farthest = [shift(far, 0, y, n_voc) for y in over_y]
    weights = (first, second)
    for blocks in ([below, *beside, above, far], [*corners, *farthest]):
        for at in range(0, len(blocks), MOST):
            sent = score(blocks[at : at + MOST], weights, sent, n_dev, per_dev)
    everything = lax.all_to_all(sent, ("tok", "voc"), 0, 0, tiled=True)
    return finish(everything, req_dev, span)


def solution(mesh):
    placed = (
        P(("tok", "voc"), None, None),
        P(),
        P(None, "voc"),
        P(("tok", "voc")),
        P(("tok", "voc")),
        P(),
        P(("tok", "voc"), None),
    )
    return jax.shard_map(
        functools.partial(shards, mesh.shape["tok"], mesh.shape["voc"]),
        mesh=mesh,
        in_specs=placed,
        out_specs=(P(("tok", "voc"), None), P(("tok", "voc"), None)),
        check_vma=False,
    )
```

```python
import functools

import jax
import jax.numpy as jnp
from jax import lax
from jax.experimental import pallas as pl
from jax.experimental.pallas import tpu as pltpu
from jax.sharding import PartitionSpec as P

EPS = 1e-06
LIVE = 24
RING = 4
LANES = 128
DIGIT = 7
NOWHERE = (1 << (2 * DIGIT)) - 1
STATS = 4
TILE = 1280
MOST = 4
CUT = 2560
PIECE = 1280
F32 = jnp.float32
BF16 = jnp.bfloat16
VMEM = pltpu.VMEM
MIB = 2**20


def iota(shape, dim):
    return lax.broadcasted_iota(jnp.int32, shape, dim)


def pack_kernel(n_voc, *refs):
    sources, out_ref, copies, sems = refs[:6], refs[6], refs[7:13], refs[13]
    started = [pltpu.make_async_copy(a, b, sems.at[at]) for at, (a, b) in enumerate(zip(sources, copies))]
    for copy in started:
        copy.start()
    for copy in started:
        copy.wait()
    offset_ref, length_ref, request_ref, hidden_ref, gain_ref, target_ref = copies
    req_dev, span, width = hidden_ref.shape
    rows = req_dev * LIVE
    device = lax.axis_index("tok") * n_voc + lax.axis_index("voc")
    values = hidden_ref[...].reshape(req_dev * span, width).astype(F32)
    square = jnp.mean(values * values, axis=-1, keepdims=True)
    normed = (values * lax.rsqrt(square + EPS) * gain_ref[...]).astype(BF16)
    row = iota((rows, 1), 0)
    source = jnp.zeros((rows, 1), jnp.int32)
    place = jnp.zeros((rows, 1), jnp.int32)
    target = jnp.zeros((rows, 1), F32)
    for slot in range(req_dev):
        step = row - slot * LIVE
        mine = (step >= 0) & (step < LIVE)
        position = offset_ref[slot] + step
        source = jnp.where(mine, slot * span + position, source)
        request = request_ref[device * req_dev + slot]
        scored = jnp.where(step < length_ref[slot], request * span + position, NOWHERE)
        place = jnp.where(mine, scored, place)
        found = mine & (iota((rows, span), 1) == position)
        ids = target_ref[slot : slot + 1, :].astype(F32)
        target += jnp.sum(jnp.where(found, ids, 0.0), axis=1, keepdims=True)
    taken = (iota((rows, req_dev * span), 1) == source).astype(BF16)
    out_ref[:, :width] = jnp.dot(taken, normed, preferred_element_type=F32).astype(BF16)
    target = target.astype(jnp.int32)
    low = (1 << DIGIT) - 1
    digits = (target >> (2 * DIGIT), (target >> DIGIT) & low, target & low, place >> DIGIT, place & low)
    lane = iota((rows, LANES), 1)
    tail = jnp.zeros((rows, LANES), jnp.int32)
    for at, digit in enumerate(digits):
        tail = jnp.where(lane == at, digit, tail)
    out_ref[:, width:] = tail.astype(F32).astype(BF16)


def pack(hidden, norm_gain, lengths, offsets, slot_request, targets, n_voc):
    req_dev, _, width = hidden.shape
    arrays = (offsets, lengths, slot_request, hidden, norm_gain.reshape(1, -1), targets)
    spaces = (pltpu.SMEM,) * 3 + (VMEM,) * 3
    return pl.pallas_call(
        functools.partial(pack_kernel, n_voc),
        out_shape=jax.ShapeDtypeStruct((req_dev * LIVE, width + LANES), BF16),
        in_specs=[pl.BlockSpec(memory_space=pl.ANY)] * 6,
        out_specs=pl.BlockSpec(memory_space=VMEM),
        scratch_shapes=[space(a.shape, a.dtype) for space, a in zip(spaces, arrays)]
        + [pltpu.SemaphoreType.DMA((6,))],
        compiler_params=pltpu.CompilerParams(vmem_limit_bytes=8 * MIB),
        name="pack",
    )(*(pltpu.with_memory_space_constraint(a, pltpu.HBM) for a in arrays))


def decode(tail):
    at, column = iota((LANES, 2 * LANES), 0), iota((LANES, 2 * LANES), 1)
    first = column < LANES
    scale = jnp.zeros((LANES, 2 * LANES), F32)
    for row, value in enumerate((1 << (2 * DIGIT), 1 << DIGIT, 1)):
        scale = jnp.where(first & (at == row), float(value), scale)
    for row, value in enumerate((1 << DIGIT, 1)):
        scale = jnp.where((~first) & (at == row + 3), float(value), scale)
    both = jnp.dot(tail, scale.astype(BF16), preferred_element_type=F32)
    return both[:, :LANES], both[:, LANES:]


def tiles(columns, size):
    return [(base, min(size, columns - base)) for base in range(0, columns, size)]


def assemble(blocks, x_ref, place_ref):
    size, width = blocks[0].shape[0], x_ref.shape[1]
    for at, block in enumerate(blocks):
        x_ref[at * size : (at + 1) * size, :] = block[:, :width]
    target, place = decode(jnp.concatenate([block[:, width:] for block in blocks], axis=0))
    place_ref[...] = place
    return target


def take(logits_ref, state, wanted, base, wide, fresh):
    peak_ref, sum_ref, dot_ref, pick_ref = state
    peak = functools.reduce(jnp.maximum, [logits_ref[:, at : at + LANES] for at in range(0, wide, LANES)])
    if fresh:
        total = dots = pick = jnp.zeros_like(peak)
    else:
        old = peak_ref[...]
        peak = jnp.maximum(old, peak)
        drop = old - peak
        scale = jnp.exp(drop)
        total = sum_ref[...]
        dots = (dot_ref[...] + drop * total) * scale
        total = total * scale
        pick = pick_ref[...]
    for at in range(0, wide, LANES):
        part = logits_ref[:, at : at + LANES]
        below = part - peak
        weight = jnp.exp(below)
        total += weight
        dots += weight * below
        pick = jnp.where(wanted == float(base + at), part, pick)
    peak_ref[...] = peak
    sum_ref[...] = total
    dot_ref[...] = dots
    pick_ref[...] = pick


def route(state, place_ref, before_ref, out_ref, per_dev):
    peak_ref, sum_ref, dot_ref, pick_ref = state
    rows = place_ref.shape[0]
    lane = iota((rows, LANES), 1).astype(F32)
    peak = jnp.max(peak_ref[...], axis=1, keepdims=True)
    drop = peak_ref[...] - peak
    scale = jnp.exp(drop)
    total = jnp.sum(sum_ref[...] * scale, axis=1, keepdims=True)
    dots = jnp.sum((dot_ref[...] + drop * sum_ref[...]) * scale, axis=1, keepdims=True)
    pick = jnp.sum(pick_ref[...], axis=1, keepdims=True)
    stats = jnp.zeros((rows, LANES), F32)
    for at, value in enumerate((peak, total, dots, pick)):
        high = value.astype(BF16).astype(F32)
        middle = (value - high).astype(BF16).astype(F32)
        low = value - high - middle
        for part, piece in enumerate((high, middle, low)):
            stats = jnp.where(lane == float(8 * part + at), piece, stats)
    stats = stats.T.astype(BF16)[:32]
    for group in range(out_ref.shape[0] * per_dev // LANES):
        there = (place_ref[...] == lane + float(group * LANES)).astype(F32).astype(BF16)
        moved = jnp.dot(stats, there, preferred_element_type=F32)
        moved = (moved[0:8] + moved[8:16] + moved[16:24])[:STATS]
        for at in range(LANES // per_dev):
            to = group * (LANES // per_dev) + at
            part = moved[:, at * per_dev : (at + 1) * per_dev]
            if before_ref is not None:
                part += before_ref[to, :, :per_dev]
            out_ref[to, :, :per_dev] = part


def sweep(x_ref, plan, logits, state, wanted):
    last = None
    for at, (weight_ref, column, base, wide, copy) in enumerate(plan):
        if copy is not None:
            copy.wait()
        logits[at % 2][:, :wide] = jnp.dot(
            x_ref[...], weight_ref[:, column : column + wide], preferred_element_type=F32
        )
        if last is not None:
            take(*last)
        last = logits[at % 2], state, wanted, base, wide, at == 0
    take(*last)


def wanted_columns(target, vocab_dev):
    first = (lax.axis_index("voc") * vocab_dev).astype(F32)
    return target - first - iota(target.shape, 1).astype(F32)


def fetch(weight_ref, held_ref, sems, lo):
    started = []
    for at, (base, wide) in enumerate(tiles(held_ref.shape[1], PIECE)):
        copy = pltpu.make_async_copy(
            weight_ref.at[:, pl.ds(lo + base, wide)], held_ref.at[:, pl.ds(base, wide)], sems.at[at]
        )
        copy.start()
        started.append((base, wide, copy))
    return started


def preload_kernel(after_ref, weight_ref, held_ref, sems):
    for _, _, copy in fetch(weight_ref, held_ref, sems, 0):
        copy.wait()


def early_kernel(count, per_dev, *refs):
    blocks, (first_ref, weight_ref, *refs) = refs[:count], refs[count:]
    out_ref, held_ref, x_ref, place_ref, even_ref, odd_ref, sems, *state = refs
    cut = first_ref.shape[1]
    copies = fetch(weight_ref, held_ref, sems, cut)
    target = assemble(blocks, x_ref, place_ref)
    plan = [(first_ref, base, base, wide, None) for base, wide in tiles(cut, TILE)]
    plan += [(held_ref, base, cut + base, wide, copy) for base, wide, copy in copies]
    sweep(x_ref, plan, (even_ref, odd_ref), state, wanted_columns(target, weight_ref.shape[1]))
    route(state, place_ref, None, out_ref, per_dev)


def late_kernel(count, per_dev, *refs):
    blocks, (first_ref, second_ref, before_ref, *refs) = refs[:count], refs[count:]
    out_ref, x_ref, place_ref, even_ref, odd_ref, *state = refs
    cut = first_ref.shape[1]
    target = assemble(blocks, x_ref, place_ref)
    plan = [(first_ref, base, base, wide, None) for base, wide in tiles(cut, TILE)]
    plan += [(second_ref, base, cut + base, wide, None) for base, wide in tiles(second_ref.shape[1], TILE)]
    sweep(x_ref, plan, (even_ref, odd_ref), state, wanted_columns(target, cut + second_ref.shape[1]))
    route(state, place_ref, before_ref, out_ref, per_dev)


def call(kernel, name, operands, spaces, out_shape, rows, wide, scratch, columns):
    specs = [pl.BlockSpec(memory_space=pl.ANY if space is pltpu.HBM else VMEM) for space in spaces]
    operands = [
        a if space is None else pltpu.with_memory_space_constraint(a, space) for a, space in zip(operands, spaces)
    ]
    width = operands[0].shape[1] - LANES
    return pl.pallas_call(
        kernel,
        out_shape=out_shape,
        in_specs=specs,
        out_specs=jax.tree.map(lambda _: pl.BlockSpec(memory_space=VMEM), out_shape),
        scratch_shapes=[VMEM((rows, width), BF16), VMEM((rows, LANES), F32)] + [VMEM((rows, wide), F32)] * 2 + scratch,
        compiler_params=pltpu.CompilerParams(vmem_limit_bytes=10 * MIB),
        cost_estimate=pl.CostEstimate(
            flops=2 * rows * width * columns, bytes_accessed=2 * width * columns, transcendentals=rows * columns
        ),
        name=name,
    )(*operands)


def preload(after, weight, cut):
    return pl.pallas_call(
        preload_kernel,
        out_shape=VMEM((weight.shape[0], cut), BF16),
        in_specs=[pl.BlockSpec(memory_space=pl.ANY)] * 2,
        out_specs=pl.BlockSpec(memory_space=VMEM),
        scratch_shapes=[pltpu.SemaphoreType.DMA((len(tiles(cut, PIECE)),))],
        compiler_params=pltpu.CompilerParams(vmem_limit_bytes=MIB),
        name="preload",
    )(after, pltpu.with_memory_space_constraint(weight, pltpu.HBM))


def early(blocks, first, weight, n_dev, per_dev):
    rows = len(blocks) * blocks[0].shape[0]
    rest = weight.shape[1] - first.shape[1]
    return call(
        functools.partial(early_kernel, len(blocks), per_dev),
        "early",
        (*blocks, first, weight),
        (VMEM,) * (len(blocks) + 1) + (pltpu.HBM,),
        (jax.ShapeDtypeStruct((n_dev, STATS, LANES), F32), VMEM((weight.shape[0], rest), BF16)),
        rows,
        TILE,
        [pltpu.SemaphoreType.DMA((len(tiles(rest, PIECE)),))] + [VMEM((rows, LANES), F32)] * STATS,
        weight.shape[1],
    )


def late(blocks, held, before, n_dev, per_dev):
    rows = len(blocks) * blocks[0].shape[0]
    return call(
        functools.partial(late_kernel, len(blocks), per_dev),
        "late",
        (*blocks, *held, before),
        (VMEM,) * (len(blocks) + 2) + (None,),
        jax.ShapeDtypeStruct((n_dev, STATS, LANES), F32),
        rows,
        TILE,
        [VMEM((rows, LANES), F32)] * STATS,
        sum(a.shape[1] for a in held),
    )


def finish_kernel(all_ref, logprob_ref, entropy_ref):
    req_dev, span = logprob_ref.shape
    peak, total, dots, pick = (all_ref[:, at, :] for at in range(4))
    held = total > 0.0
    top = jnp.max(jnp.where(held, peak, -jnp.inf), axis=0, keepdims=True)
    scored = top > -jnp.inf
    top = jnp.where(scored, top, 0.0)
    drop = jnp.where(held, peak - top, 0.0)
    scale = jnp.exp(drop)
    whole = jnp.sum(total * scale, axis=0, keepdims=True)
    whole = jnp.where(scored, whole, 1.0)
    mean = jnp.sum((dots + drop * total) * scale, axis=0, keepdims=True) / whole
    log_total = jnp.log(whole)
    logprob = jnp.where(scored, jnp.sum(pick, axis=0, keepdims=True) - top - log_total, 0.0)
    entropy = jnp.where(scored, log_total - mean, 0.0)
    for at in range(req_dev):
        logprob_ref[at : at + 1, :] = logprob[:, at * span : (at + 1) * span]
        entropy_ref[at : at + 1, :] = entropy[:, at * span : (at + 1) * span]


def finish(everything, req_dev, span):
    vmem = pl.BlockSpec(memory_space=VMEM)
    shape = jax.ShapeDtypeStruct((req_dev, span), F32)
    return pl.pallas_call(
        finish_kernel,
        out_shape=(shape, shape),
        in_specs=[vmem],
        out_specs=(vmem, vmem),
        compiler_params=pltpu.CompilerParams(vmem_limit_bytes=8 * MIB),
        name="finish",
    )(everything)


def shift(block, along_z, along_y, n_voc):
    side = n_voc // RING
    pairs = [
        (z * side + y, (z + along_z) % RING * side + (y + along_y) % side)
        for z in range(RING)
        for y in range(side)
    ]
    return lax.ppermute(block, "voc", pairs)


def shards(n_tok, n_voc, hidden, norm_gain, head_weight, lengths, offsets, slot_request, targets):
    req_dev, span, _ = hidden.shape
    n_dev, per_dev = n_tok * n_voc, req_dev * span
    over_y = range(1, n_voc // RING)
    own = pack(hidden, norm_gain, lengths, offsets, slot_request, targets, n_voc)
    below = shift(own, -1, 0, n_voc)
    beside = [shift(own, 0, y, n_voc) for y in over_y]
    above = shift(own, 1, 0, n_voc)
    left = preload(own, head_weight, CUT)
    left, below = lax.optimization_barrier((left, below))
    far = [shift(below, -1, y, n_voc) for y in range(n_voc // RING)]
    corners = [shift(a, 0, y, n_voc) for y in over_y for a in (below, above)]
    sent, right = early([own, below, *beside, above][:MOST], left, head_weight, n_dev, per_dev)
    rest = [own, below, *beside, above][MOST:] + [*corners, *far]
    for at in range(0, len(rest), MOST):
        sent = late(rest[at : at + MOST], (left, right), sent, n_dev, per_dev)
    everything = lax.all_to_all(sent, ("tok", "voc"), 0, 0, tiled=True)
    return finish(everything, req_dev, span)


def solution(mesh):
    placed = (
        P(("tok", "voc"), None, None),
        P(),
        P(None, "voc"),
        P(("tok", "voc")),
        P(("tok", "voc")),
        P(),
        P(("tok", "voc"), None),
    )
    return jax.shard_map(
        functools.partial(shards, mesh.shape["tok"], mesh.shape["voc"]),
        mesh=mesh,
        in_specs=placed,
        out_specs=(P(("tok", "voc"), None), P(("tok", "voc"), None)),
        check_vma=False,
    )
```

```python
import functools

import jax
import jax.numpy as jnp
from jax import lax
from jax.experimental import pallas as pl
from jax.experimental.pallas import tpu as pltpu
from jax.sharding import PartitionSpec as P

EPS = 1e-06
LIVE = 24
RING = 4
LANES = 128
DIGIT = 7
TAIL = 16
NOWHERE = (1 << (2 * DIGIT)) - 1
STATS = 4
TILE = 1280
MOST = 4
CUT = 2560
PIECE = 1280
F32 = jnp.float32
BF16 = jnp.bfloat16
VMEM = pltpu.VMEM
MIB = 2**20


def iota(shape, dim):
    return lax.broadcasted_iota(jnp.int32, shape, dim)


def pack_kernel(n_voc, *refs):
    sources, out_ref, copies, sems = refs[:6], refs[6], refs[7:13], refs[13]
    started = [pltpu.make_async_copy(a, b, sems.at[at]) for at, (a, b) in enumerate(zip(sources, copies))]
    for copy in started:
        copy.start()
    for copy in started:
        copy.wait()
    offset_ref, length_ref, request_ref, hidden_ref, gain_ref, target_ref = copies
    req_dev, span, width = hidden_ref.shape
    rows = req_dev * LIVE
    device = lax.axis_index("tok") * n_voc + lax.axis_index("voc")
    values = hidden_ref[...].reshape(req_dev * span, width).astype(F32)
    square = jnp.mean(values * values, axis=-1, keepdims=True)
    normed = (values * lax.rsqrt(square + EPS) * gain_ref[...]).astype(BF16)

    def window(row):
        source = place = jnp.zeros(row.shape, jnp.int32) + NOWHERE
        for slot in range(req_dev):
            step = row - slot * LIVE
            mine = (step >= 0) & (step < LIVE)
            position = offset_ref[slot] + step
            request = request_ref[device * req_dev + slot]
            source = jnp.where(mine, slot * span + position, source)
            place = jnp.where(mine & (step < length_ref[slot]), request * span + position, place)
        return source, place

    source, _ = window(iota((rows, 1), 0))
    taken = (iota((rows, req_dev * span), 1) == source).astype(BF16)
    sent = jnp.dot(taken, normed, preferred_element_type=F32).astype(BF16)
    for at in range(width // LANES):
        out_ref[at * rows : (at + 1) * rows, :] = sent[:, at * LANES : (at + 1) * LANES]
    source, place = window(iota((1, LANES), 1))
    taken = (iota((req_dev * span, LANES), 0) == source).astype(BF16)
    target = jnp.concatenate([target_ref[slot : slot + 1, :] for slot in range(req_dev)], axis=1)
    low = (1 << DIGIT) - 1
    kind = iota((TAIL, req_dev * span), 0)
    digits = jnp.zeros((TAIL, req_dev * span), jnp.int32)
    for at, digit in enumerate((target >> (2 * DIGIT), (target >> DIGIT) & low, target & low)):
        digits = jnp.where(kind == at, digit, digits)
    tail = jnp.dot(digits.astype(F32).astype(BF16), taken, preferred_element_type=F32)
    kind = iota((TAIL, LANES), 0)
    for at, digit in enumerate((place >> DIGIT, place & low)):
        tail = jnp.where(kind == at + 3, digit.astype(F32), tail)
    out_ref[width // LANES * rows :, :] = tail.astype(BF16)


def pack(hidden, norm_gain, lengths, offsets, slot_request, targets, n_voc):
    req_dev, _, width = hidden.shape
    arrays = (offsets, lengths, slot_request, hidden, norm_gain.reshape(1, -1), targets)
    spaces = (pltpu.SMEM,) * 3 + (VMEM,) * 3
    return pl.pallas_call(
        functools.partial(pack_kernel, n_voc),
        out_shape=jax.ShapeDtypeStruct((width // LANES * req_dev * LIVE + TAIL, LANES), BF16),
        in_specs=[pl.BlockSpec(memory_space=pl.ANY)] * 6,
        out_specs=pl.BlockSpec(memory_space=VMEM),
        scratch_shapes=[space(a.shape, a.dtype) for space, a in zip(spaces, arrays)]
        + [pltpu.SemaphoreType.DMA((6,))],
        compiler_params=pltpu.CompilerParams(vmem_limit_bytes=8 * MIB),
        name="pack",
    )(*(pltpu.with_memory_space_constraint(a, pltpu.HBM) for a in arrays))


def decode(tail):
    at, column = iota((TAIL, 2 * LANES), 0), iota((TAIL, 2 * LANES), 1)
    scale = jnp.zeros((TAIL, 2 * LANES), F32)
    for row, value in enumerate((1 << (2 * DIGIT), 1 << DIGIT, 1, 1 << DIGIT, 1)):
        scale = jnp.where((at == row) & ((column < LANES) == (row < 3)), float(value), scale)
    both = lax.dot_general(tail, scale.astype(BF16), (((0,), (0,)), ((), ())), preferred_element_type=F32)
    return both[:, :LANES], both[:, LANES:]


def tiles(columns, size):
    return [(base, min(size, columns - base)) for base in range(0, columns, size)]


def height(block, width):
    return (block.shape[0] - TAIL) * LANES // width


def assemble(blocks, x_ref, place_ref):
    width = x_ref.shape[1]
    size = height(blocks[0], width)
    targets = []
    for at, block in enumerate(blocks):
        rows = slice(at * size, (at + 1) * size)
        for part in range(width // LANES):
            x_ref[rows, part * LANES : (part + 1) * LANES] = block[part * size : (part + 1) * size, :]
        target, place = decode(block[width // LANES * size :, :])
        place_ref[rows, :] = place[:size]
        targets.append(target[:size])
    return jnp.concatenate(targets, axis=0)


def take(logits_ref, state, wanted, base, wide, fresh):
    peak_ref, sum_ref, dot_ref, pick_ref = state
    peak = functools.reduce(jnp.maximum, [logits_ref[:, at : at + LANES] for at in range(0, wide, LANES)])
    if fresh:
        total = dots = pick = jnp.zeros_like(peak)
    else:
        old = peak_ref[...]
        peak = jnp.maximum(old, peak)
        drop = old - peak
        scale = jnp.exp(drop)
        total = sum_ref[...]
        dots = (dot_ref[...] + drop * total) * scale
        total = total * scale
        pick = pick_ref[...]
    for at in range(0, wide, LANES):
        part = logits_ref[:, at : at + LANES]
        below = part - peak
        weight = jnp.exp(below)
        total += weight
        dots += weight * below
        pick = jnp.where(wanted == float(base + at), part, pick)
    peak_ref[...] = peak
    sum_ref[...] = total
    dot_ref[...] = dots
    pick_ref[...] = pick


def route(state, place_ref, before_ref, out_ref, per_dev):
    peak_ref, sum_ref, dot_ref, pick_ref = state
    rows = place_ref.shape[0]
    lane = iota((rows, LANES), 1).astype(F32)
    peak = jnp.max(peak_ref[...], axis=1, keepdims=True)
    drop = peak_ref[...] - peak
    scale = jnp.exp(drop)
    total = jnp.sum(sum_ref[...] * scale, axis=1, keepdims=True)
    dots = jnp.sum((dot_ref[...] + drop * sum_ref[...]) * scale, axis=1, keepdims=True)
    pick = jnp.sum(pick_ref[...], axis=1, keepdims=True)
    stats = jnp.zeros((rows, LANES), F32)
    for at, value in enumerate((peak, total, dots, pick)):
        high = value.astype(BF16).astype(F32)
        middle = (value - high).astype(BF16).astype(F32)
        low = value - high - middle
        for part, piece in enumerate((high, middle, low)):
            stats = jnp.where(lane == float(8 * part + at), piece, stats)
    stats = stats.T.astype(BF16)[:32]
    for group in range(out_ref.shape[0] * per_dev // LANES):
        there = (place_ref[...] == lane + float(group * LANES)).astype(F32).astype(BF16)
        moved = jnp.dot(stats, there, preferred_element_type=F32)
        moved = (moved[0:8] + moved[8:16] + moved[16:24])[:STATS]
        for at in range(LANES // per_dev):
            to = group * (LANES // per_dev) + at
            part = moved[:, at * per_dev : (at + 1) * per_dev]
            if before_ref is not None:
                part += before_ref[to, :, :per_dev]
            out_ref[to, :, :per_dev] = part


def sweep(x_ref, plan, logits, state, wanted):
    last = None
    for at, (weight_ref, column, base, wide, copy) in enumerate(plan):
        if copy is not None:
            copy.wait()
        logits[at % 2][:, :wide] = jnp.dot(
            x_ref[...], weight_ref[:, column : column + wide], preferred_element_type=F32
        )
        if last is not None:
            take(*last)
        last = logits[at % 2], state, wanted, base, wide, at == 0
    take(*last)


def wanted_columns(target, vocab_dev):
    first = (lax.axis_index("voc") * vocab_dev).astype(F32)
    return target - first - iota(target.shape, 1).astype(F32)


def fetch(weight_ref, held_ref, sems, lo):
    started = []
    for at, (base, wide) in enumerate(tiles(held_ref.shape[1], PIECE)):
        copy = pltpu.make_async_copy(
            weight_ref.at[:, pl.ds(lo + base, wide)], held_ref.at[:, pl.ds(base, wide)], sems.at[at]
        )
        copy.start()
        started.append((base, wide, copy))
    return started


def preload_kernel(after_ref, weight_ref, held_ref, sems):
    for _, _, copy in fetch(weight_ref, held_ref, sems, 0):
        copy.wait()


def early_kernel(count, per_dev, *refs):
    blocks, (first_ref, weight_ref, *refs) = refs[:count], refs[count:]
    out_ref, held_ref, x_ref, place_ref, even_ref, odd_ref, sems, *state = refs
    cut = first_ref.shape[1]
    copies = fetch(weight_ref, held_ref, sems, cut)
    target = assemble(blocks, x_ref, place_ref)
    plan = [(first_ref, base, base, wide, None) for base, wide in tiles(cut, TILE)]
    plan += [(held_ref, base, cut + base, wide, copy) for base, wide, copy in copies]
    sweep(x_ref, plan, (even_ref, odd_ref), state, wanted_columns(target, weight_ref.shape[1]))
    route(state, place_ref, None, out_ref, per_dev)


def late_kernel(count, per_dev, *refs):
    blocks, (first_ref, second_ref, before_ref, *refs) = refs[:count], refs[count:]
    out_ref, x_ref, place_ref, even_ref, odd_ref, *state = refs
    cut = first_ref.shape[1]
    target = assemble(blocks, x_ref, place_ref)
    plan = [(first_ref, base, base, wide, None) for base, wide in tiles(cut, TILE)]
    plan += [(second_ref, base, cut + base, wide, None) for base, wide in tiles(second_ref.shape[1], TILE)]
    sweep(x_ref, plan, (even_ref, odd_ref), state, wanted_columns(target, cut + second_ref.shape[1]))
    route(state, place_ref, before_ref, out_ref, per_dev)


def call(kernel, name, operands, spaces, out_shape, rows, width, scratch, columns):
    specs = [pl.BlockSpec(memory_space=pl.ANY if space is pltpu.HBM else VMEM) for space in spaces]
    operands = [
        a if space is None else pltpu.with_memory_space_constraint(a, space) for a, space in zip(operands, spaces)
    ]
    return pl.pallas_call(
        kernel,
        out_shape=out_shape,
        in_specs=specs,
        out_specs=jax.tree.map(lambda _: pl.BlockSpec(memory_space=VMEM), out_shape),
        scratch_shapes=[VMEM((rows, width), BF16), VMEM((rows, LANES), F32)] + [VMEM((rows, TILE), F32)] * 2 + scratch,
        compiler_params=pltpu.CompilerParams(vmem_limit_bytes=10 * MIB),
        cost_estimate=pl.CostEstimate(
            flops=2 * rows * width * columns, bytes_accessed=2 * width * columns, transcendentals=rows * columns
        ),
        name=name,
    )(*operands)


def preload(after, weight, cut):
    return pl.pallas_call(
        preload_kernel,
        out_shape=VMEM((weight.shape[0], cut), BF16),
        in_specs=[pl.BlockSpec(memory_space=pl.ANY)] * 2,
        out_specs=pl.BlockSpec(memory_space=VMEM),
        scratch_shapes=[pltpu.SemaphoreType.DMA((len(tiles(cut, PIECE)),))],
        compiler_params=pltpu.CompilerParams(vmem_limit_bytes=MIB),
        name="preload",
    )(after, pltpu.with_memory_space_constraint(weight, pltpu.HBM))


def early(blocks, first, weight, n_dev, per_dev):
    width = weight.shape[0]
    rows = len(blocks) * height(blocks[0], width)
    rest = weight.shape[1] - first.shape[1]
    return call(
        functools.partial(early_kernel, len(blocks), per_dev),
        "early",
        (*blocks, first, weight),
        (VMEM,) * (len(blocks) + 1) + (pltpu.HBM,),
        (jax.ShapeDtypeStruct((n_dev, STATS, LANES), F32), VMEM((width, rest), BF16)),
        rows,
        width,
        [pltpu.SemaphoreType.DMA((len(tiles(rest, PIECE)),))] + [VMEM((rows, LANES), F32)] * STATS,
        weight.shape[1],
    )


def late(blocks, held, before, n_dev, per_dev):
    width = held[0].shape[0]
    rows = len(blocks) * height(blocks[0], width)
    return call(
        functools.partial(late_kernel, len(blocks), per_dev),
        "late",
        (*blocks, *held, before),
        (VMEM,) * (len(blocks) + 2) + (None,),
        jax.ShapeDtypeStruct((n_dev, STATS, LANES), F32),
        rows,
        width,
        [VMEM((rows, LANES), F32)] * STATS,
        sum(a.shape[1] for a in held),
    )


def finish_kernel(all_ref, logprob_ref, entropy_ref):
    req_dev, span = logprob_ref.shape
    peak, total, dots, pick = (all_ref[:, at, :] for at in range(4))
    held = total > 0.0
    top = jnp.max(jnp.where(held, peak, -jnp.inf), axis=0, keepdims=True)
    scored = top > -jnp.inf
    top = jnp.where(scored, top, 0.0)
    drop = jnp.where(held, peak - top, 0.0)
    scale = jnp.exp(drop)
    whole = jnp.sum(total * scale, axis=0, keepdims=True)
    whole = jnp.where(scored, whole, 1.0)
    mean = jnp.sum((dots + drop * total) * scale, axis=0, keepdims=True) / whole
    log_total = jnp.log(whole)
    logprob = jnp.where(scored, jnp.sum(pick, axis=0, keepdims=True) - top - log_total, 0.0)
    entropy = jnp.where(scored, log_total - mean, 0.0)
    for at in range(req_dev):
        logprob_ref[at : at + 1, :] = logprob[:, at * span : (at + 1) * span]
        entropy_ref[at : at + 1, :] = entropy[:, at * span : (at + 1) * span]


def finish(everything, req_dev, span):
    vmem = pl.BlockSpec(memory_space=VMEM)
    shape = jax.ShapeDtypeStruct((req_dev, span), F32)
    return pl.pallas_call(
        finish_kernel,
        out_shape=(shape, shape),
        in_specs=[vmem],
        out_specs=(vmem, vmem),
        compiler_params=pltpu.CompilerParams(vmem_limit_bytes=8 * MIB),
        name="finish",
    )(everything)


def shift(block, along_z, along_y, n_voc):
    side = n_voc // RING
    pairs = [
        (z * side + y, (z + along_z) % RING * side + (y + along_y) % side)
        for z in range(RING)
        for y in range(side)
    ]
    return lax.ppermute(block, "voc", pairs)


def shards(n_tok, n_voc, hidden, norm_gain, head_weight, lengths, offsets, slot_request, targets):
    req_dev, span, _ = hidden.shape
    n_dev, per_dev = n_tok * n_voc, req_dev * span
    over_y = range(1, n_voc // RING)
    own = pack(hidden, norm_gain, lengths, offsets, slot_request, targets, n_voc)
    below = shift(own, -1, 0, n_voc)
    beside = [shift(own, 0, y, n_voc) for y in over_y]
    above = shift(own, 1, 0, n_voc)
    left = preload(own, head_weight, CUT)
    left, below = lax.optimization_barrier((left, below))
    far = [shift(below, -1, y, n_voc) for y in range(n_voc // RING)]
    corners = [shift(a, 0, y, n_voc) for y in over_y for a in (below, above)]
    sent, right = early([own, below, *beside, above][:MOST], left, head_weight, n_dev, per_dev)
    rest = [own, below, *beside, above][MOST:] + [*corners, *far]
    for at in range(0, len(rest), MOST):
        sent = late(rest[at : at + MOST], (left, right), sent, n_dev, per_dev)
    everything = lax.all_to_all(sent, ("tok", "voc"), 0, 0, tiled=True)
    return finish(everything, req_dev, span)


def solution(mesh):
    placed = (
        P(("tok", "voc"), None, None),
        P(),
        P(None, "voc"),
        P(("tok", "voc")),
        P(("tok", "voc")),
        P(),
        P(("tok", "voc"), None),
    )
    return jax.shard_map(
        functools.partial(shards, mesh.shape["tok"], mesh.shape["voc"]),
        mesh=mesh,
        in_specs=placed,
        out_specs=(P(("tok", "voc"), None), P(("tok", "voc"), None)),
        check_vma=False,
    )
```

```python
import functools

import jax
import jax.numpy as jnp
from jax import lax
from jax.experimental import pallas as pl
from jax.experimental.pallas import tpu as pltpu
from jax.sharding import PartitionSpec as P

EPS = 1e-06
LIVE = 24
RING = 4
LANES = 128
DIGIT = 7
TAIL = 16
NOWHERE = (1 << (2 * DIGIT)) - 1
STATS = 4
TILE = 1280
SHORT = 512
MOST = 4
CUT = 2560
PIECE = 1280
F32 = jnp.float32
BF16 = jnp.bfloat16
VMEM = pltpu.VMEM
MIB = 2**20


def iota(shape, dim):
    return lax.broadcasted_iota(jnp.int32, shape, dim)


def pack_kernel(n_voc, *refs):
    sources, out_ref, copies, sems = refs[:6], refs[6], refs[7:13], refs[13]
    started = [pltpu.make_async_copy(a, b, sems.at[at]) for at, (a, b) in enumerate(zip(sources, copies))]
    for copy in started:
        copy.start()
    for copy in started:
        copy.wait()
    offset_ref, length_ref, request_ref, hidden_ref, gain_ref, target_ref = copies
    req_dev, span, width = hidden_ref.shape
    rows = req_dev * LIVE
    device = lax.axis_index("tok") * n_voc + lax.axis_index("voc")
    values = hidden_ref[...].reshape(req_dev * span, width).astype(F32)
    square = jnp.mean(values * values, axis=-1, keepdims=True)
    normed = (values * lax.rsqrt(square + EPS) * gain_ref[...]).astype(BF16)

    def window(row):
        source = place = jnp.zeros(row.shape, jnp.int32) + NOWHERE
        for slot in range(req_dev):
            step = row - slot * LIVE
            mine = (step >= 0) & (step < LIVE)
            position = offset_ref[slot] + step
            request = request_ref[device * req_dev + slot]
            source = jnp.where(mine, slot * span + position, source)
            place = jnp.where(mine & (step < length_ref[slot]), request * span + position, place)
        return source, place

    source, _ = window(iota((rows, 1), 0))
    taken = (iota((rows, req_dev * span), 1) == source).astype(BF16)
    sent = jnp.dot(taken, normed, preferred_element_type=F32).astype(BF16)
    for at in range(width // LANES):
        out_ref[at * rows : (at + 1) * rows, :] = sent[:, at * LANES : (at + 1) * LANES]
    source, place = window(iota((1, LANES), 1))
    taken = (iota((req_dev * span, LANES), 0) == source).astype(BF16)
    target = jnp.concatenate([target_ref[slot : slot + 1, :] for slot in range(req_dev)], axis=1)
    low = (1 << DIGIT) - 1
    kind = iota((TAIL, req_dev * span), 0)
    digits = jnp.zeros((TAIL, req_dev * span), jnp.int32)
    for at, digit in enumerate((target >> (2 * DIGIT), (target >> DIGIT) & low, target & low)):
        digits = jnp.where(kind == at, digit, digits)
    tail = jnp.dot(digits.astype(F32).astype(BF16), taken, preferred_element_type=F32)
    kind = iota((TAIL, LANES), 0)
    for at, digit in enumerate((place >> DIGIT, place & low)):
        tail = jnp.where(kind == at + 3, digit.astype(F32), tail)
    out_ref[width // LANES * rows :, :] = tail.astype(BF16)


def pack(hidden, norm_gain, lengths, offsets, slot_request, targets, n_voc):
    req_dev, _, width = hidden.shape
    arrays = (offsets, lengths, slot_request, hidden, norm_gain.reshape(1, -1), targets)
    spaces = (pltpu.SMEM,) * 3 + (VMEM,) * 3
    return pl.pallas_call(
        functools.partial(pack_kernel, n_voc),
        out_shape=jax.ShapeDtypeStruct((width // LANES * req_dev * LIVE + TAIL, LANES), BF16),
        in_specs=[pl.BlockSpec(memory_space=pl.ANY)] * 6,
        out_specs=pl.BlockSpec(memory_space=VMEM),
        scratch_shapes=[space(a.shape, a.dtype) for space, a in zip(spaces, arrays)]
        + [pltpu.SemaphoreType.DMA((6,))],
        compiler_params=pltpu.CompilerParams(vmem_limit_bytes=8 * MIB),
        name="pack",
    )(*(pltpu.with_memory_space_constraint(a, pltpu.HBM) for a in arrays))


def decode(tail):
    at, column = iota((TAIL, 2 * LANES), 0), iota((TAIL, 2 * LANES), 1)
    scale = jnp.zeros((TAIL, 2 * LANES), F32)
    for row, value in enumerate((1 << (2 * DIGIT), 1 << DIGIT, 1, 1 << DIGIT, 1)):
        scale = jnp.where((at == row) & ((column < LANES) == (row < 3)), float(value), scale)
    both = lax.dot_general(tail, scale.astype(BF16), (((0,), (0,)), ((), ())), preferred_element_type=F32)
    return both[:, :LANES], both[:, LANES:]


def tiles(columns, size):
    return [(base, min(size, columns - base)) for base in range(0, columns, size)]


def shorten(plan):
    *plan, (weight_ref, column, base, wide, copy) = plan
    cut = max(wide - SHORT, 0)
    head = [(weight_ref, column, base, cut, copy)] if cut else []
    return plan + head + [(weight_ref, column + cut, base + cut, wide - cut, None if cut else copy)]


def height(block, width):
    return (block.shape[0] - TAIL) * LANES // width


def assemble(blocks, x_ref, place_ref):
    width = x_ref.shape[1]
    size = height(blocks[0], width)
    targets = []
    for at, block in enumerate(blocks):
        rows = slice(at * size, (at + 1) * size)
        for part in range(width // LANES):
            x_ref[rows, part * LANES : (part + 1) * LANES] = block[part * size : (part + 1) * size, :]
        target, place = decode(block[width // LANES * size :, :])
        place_ref[rows, :] = place[:size]
        targets.append(target[:size])
    return jnp.concatenate(targets, axis=0)


def take(logits_ref, state, wanted, base, wide, fresh):
    peak_ref, sum_ref, dot_ref, pick_ref = state
    peak = functools.reduce(jnp.maximum, [logits_ref[:, at : at + LANES] for at in range(0, wide, LANES)])
    if fresh:
        total = dots = pick = jnp.zeros_like(peak)
    else:
        old = peak_ref[...]
        peak = jnp.maximum(old, peak)
        drop = old - peak
        scale = jnp.exp(drop)
        total = sum_ref[...]
        dots = (dot_ref[...] + drop * total) * scale
        total = total * scale
        pick = pick_ref[...]
    for at in range(0, wide, LANES):
        part = logits_ref[:, at : at + LANES]
        below = part - peak
        weight = jnp.exp(below)
        total += weight
        dots += weight * below
        pick = jnp.where(wanted == float(base + at), part, pick)
    peak_ref[...] = peak
    sum_ref[...] = total
    dot_ref[...] = dots
    pick_ref[...] = pick


def route(state, place_ref, before_ref, out_ref, span, per_dev):
    peak_ref, sum_ref, dot_ref, pick_ref = state
    rows = place_ref.shape[0]
    shift = span.bit_length() - 1
    lane = iota((rows, LANES), 1).astype(F32)
    peak = jnp.max(peak_ref[...], axis=1, keepdims=True)
    drop = peak_ref[...] - peak
    scale = jnp.exp(drop)
    total = jnp.sum(sum_ref[...] * scale, axis=1, keepdims=True)
    dots = jnp.sum((dot_ref[...] + drop * sum_ref[...]) * scale, axis=1, keepdims=True)
    pick = jnp.sum(pick_ref[...], axis=1, keepdims=True)
    stats = jnp.zeros((rows, LANES), F32)
    for at, value in enumerate((peak, total, dots, pick)):
        high = value.astype(BF16).astype(F32)
        middle = (value - high).astype(BF16).astype(F32)
        low = value - high - middle
        for part, piece in enumerate((high, middle, low)):
            stats = jnp.where(lane == float(8 * part + at), piece, stats)
    stats = stats.T.astype(BF16)[:32]
    lane = iota((STATS, LANES), 1)
    slots = []
    for first_row in range(0, rows, LIVE):
        request = jnp.broadcast_to(place_ref[first_row : first_row + 1, :].astype(jnp.int32) >> shift, (STATS, LANES))
        spot = (request * span + (lane & (span - 1))).astype(F32)[:1]
        there = (place_ref[...] == spot).astype(F32).astype(BF16)
        moved = jnp.dot(stats, there, preferred_element_type=F32)
        slots.append((request, (moved[0:8] + moved[8:16] + moved[16:24])[:STATS]))
    for group in range(out_ref.shape[0] * per_dev // LANES):
        held = group * (LANES // span) + (lane >> shift)
        total = jnp.zeros((STATS, LANES), F32)
        for request, moved in slots:
            total = jnp.where(request == held, moved, total)
        for at in range(LANES // per_dev):
            to = group * (LANES // per_dev) + at
            part = total[:, at * per_dev : (at + 1) * per_dev]
            if before_ref is not None:
                part += before_ref[to, :, :per_dev]
            out_ref[to, :, :per_dev] = part


def sweep(x_ref, plan, logits, state, wanted):
    last = None
    for at, (weight_ref, column, base, wide, copy) in enumerate(plan):
        if copy is not None:
            copy.wait()
        logits[at % 2][:, :wide] = jnp.dot(
            x_ref[...], weight_ref[:, column : column + wide], preferred_element_type=F32
        )
        if last is not None:
            take(*last)
        last = logits[at % 2], state, wanted, base, wide, at == 0
    take(*last)


def wanted_columns(target, vocab_dev):
    first = (lax.axis_index("voc") * vocab_dev).astype(F32)
    return target - first - iota(target.shape, 1).astype(F32)


def fetch(weight_ref, held_ref, sems, lo):
    started = []
    for at, (base, wide) in enumerate(tiles(held_ref.shape[1], PIECE)):
        copy = pltpu.make_async_copy(
            weight_ref.at[:, pl.ds(lo + base, wide)], held_ref.at[:, pl.ds(base, wide)], sems.at[at]
        )
        copy.start()
        started.append((base, wide, copy))
    return started


def preload_kernel(after_ref, weight_ref, held_ref, sems):
    for _, _, copy in fetch(weight_ref, held_ref, sems, 0):
        copy.wait()


def early_kernel(count, span, per_dev, *refs):
    blocks, (first_ref, weight_ref, *refs) = refs[:count], refs[count:]
    out_ref, held_ref, x_ref, place_ref, even_ref, odd_ref, sems, *state = refs
    cut = first_ref.shape[1]
    copies = fetch(weight_ref, held_ref, sems, cut)
    target = assemble(blocks, x_ref, place_ref)
    plan = [(first_ref, base, base, wide, None) for base, wide in tiles(cut, TILE)]
    plan += [(held_ref, base, cut + base, wide, copy) for base, wide, copy in copies]
    sweep(x_ref, shorten(plan), (even_ref, odd_ref), state, wanted_columns(target, weight_ref.shape[1]))
    route(state, place_ref, None, out_ref, span, per_dev)


def late_kernel(count, span, per_dev, *refs):
    blocks, (first_ref, second_ref, before_ref, *refs) = refs[:count], refs[count:]
    out_ref, x_ref, place_ref, even_ref, odd_ref, *state = refs
    cut = first_ref.shape[1]
    target = assemble(blocks, x_ref, place_ref)
    plan = [(first_ref, base, base, wide, None) for base, wide in tiles(cut, TILE)]
    plan += [(second_ref, base, cut + base, wide, None) for base, wide in tiles(second_ref.shape[1], TILE)]
    sweep(x_ref, shorten(plan), (even_ref, odd_ref), state, wanted_columns(target, cut + second_ref.shape[1]))
    route(state, place_ref, before_ref, out_ref, span, per_dev)


def call(kernel, name, operands, spaces, out_shape, rows, width, scratch, columns):
    specs = [pl.BlockSpec(memory_space=pl.ANY if space is pltpu.HBM else VMEM) for space in spaces]
    operands = [
        a if space is None else pltpu.with_memory_space_constraint(a, space) for a, space in zip(operands, spaces)
    ]
    return pl.pallas_call(
        kernel,
        out_shape=out_shape,
        in_specs=specs,
        out_specs=jax.tree.map(lambda _: pl.BlockSpec(memory_space=VMEM), out_shape),
        scratch_shapes=[VMEM((rows, width), BF16), VMEM((rows, LANES), F32)] + [VMEM((rows, TILE), F32)] * 2 + scratch,
        compiler_params=pltpu.CompilerParams(vmem_limit_bytes=10 * MIB),
        cost_estimate=pl.CostEstimate(
            flops=2 * rows * width * columns, bytes_accessed=2 * width * columns, transcendentals=rows * columns
        ),
        name=name,
    )(*operands)


def preload(after, weight, cut):
    return pl.pallas_call(
        preload_kernel,
        out_shape=VMEM((weight.shape[0], cut), BF16),
        in_specs=[pl.BlockSpec(memory_space=pl.ANY)] * 2,
        out_specs=pl.BlockSpec(memory_space=VMEM),
        scratch_shapes=[pltpu.SemaphoreType.DMA((len(tiles(cut, PIECE)),))],
        compiler_params=pltpu.CompilerParams(vmem_limit_bytes=MIB),
        name="preload",
    )(after, pltpu.with_memory_space_constraint(weight, pltpu.HBM))


def early(blocks, first, weight, n_dev, span, per_dev):
    width = weight.shape[0]
    rows = len(blocks) * height(blocks[0], width)
    rest = weight.shape[1] - first.shape[1]
    return call(
        functools.partial(early_kernel, len(blocks), span, per_dev),
        "early",
        (*blocks, first, weight),
        (VMEM,) * (len(blocks) + 1) + (pltpu.HBM,),
        (jax.ShapeDtypeStruct((n_dev, STATS, LANES), F32), VMEM((width, rest), BF16)),
        rows,
        width,
        [pltpu.SemaphoreType.DMA((len(tiles(rest, PIECE)),))] + [VMEM((rows, LANES), F32)] * STATS,
        weight.shape[1],
    )


def late(blocks, held, before, n_dev, span, per_dev):
    width = held[0].shape[0]
    rows = len(blocks) * height(blocks[0], width)
    return call(
        functools.partial(late_kernel, len(blocks), span, per_dev),
        "late",
        (*blocks, *held, before),
        (VMEM,) * (len(blocks) + 2) + (None,),
        jax.ShapeDtypeStruct((n_dev, STATS, LANES), F32),
        rows,
        width,
        [VMEM((rows, LANES), F32)] * STATS,
        sum(a.shape[1] for a in held),
    )


def finish_kernel(all_ref, logprob_ref, entropy_ref):
    req_dev, span = logprob_ref.shape
    peak, total, dots, pick = (all_ref[:, at, :] for at in range(4))
    held = total > 0.0
    top = jnp.max(jnp.where(held, peak, -jnp.inf), axis=0, keepdims=True)
    scored = top > -jnp.inf
    top = jnp.where(scored, top, 0.0)
    drop = jnp.where(held, peak - top, 0.0)
    scale = jnp.exp(drop)
    whole = jnp.sum(total * scale, axis=0, keepdims=True)
    whole = jnp.where(scored, whole, 1.0)
    mean = jnp.sum((dots + drop * total) * scale, axis=0, keepdims=True) / whole
    log_total = jnp.log(whole)
    logprob = jnp.where(scored, jnp.sum(pick, axis=0, keepdims=True) - top - log_total, 0.0)
    entropy = jnp.where(scored, log_total - mean, 0.0)
    for at in range(req_dev):
        logprob_ref[at : at + 1, :] = logprob[:, at * span : (at + 1) * span]
        entropy_ref[at : at + 1, :] = entropy[:, at * span : (at + 1) * span]


def finish(everything, req_dev, span):
    vmem = pl.BlockSpec(memory_space=VMEM)
    shape = jax.ShapeDtypeStruct((req_dev, span), F32)
    return pl.pallas_call(
        finish_kernel,
        out_shape=(shape, shape),
        in_specs=[vmem],
        out_specs=(vmem, vmem),
        compiler_params=pltpu.CompilerParams(vmem_limit_bytes=8 * MIB),
        name="finish",
    )(everything)


def shift(block, along_z, along_y, n_voc):
    side = n_voc // RING
    pairs = [
        (z * side + y, (z + along_z) % RING * side + (y + along_y) % side)
        for z in range(RING)
        for y in range(side)
    ]
    return lax.ppermute(block, "voc", pairs)


def shards(n_tok, n_voc, hidden, norm_gain, head_weight, lengths, offsets, slot_request, targets):
    req_dev, span, _ = hidden.shape
    n_dev, per_dev = n_tok * n_voc, req_dev * span
    over_y = range(1, n_voc // RING)
    own = pack(hidden, norm_gain, lengths, offsets, slot_request, targets, n_voc)
    below = shift(own, -1, 0, n_voc)
    beside = [shift(own, 0, y, n_voc) for y in over_y]
    above = shift(own, 1, 0, n_voc)
    left = preload(own, head_weight, CUT)
    left, below = lax.optimization_barrier((left, below))
    far = [shift(below, -1, y, n_voc) for y in range(n_voc // RING)]
    corners = [shift(a, 0, y, n_voc) for y in over_y for a in (below, above)]
    sent, right = early([own, below, *beside, above][:MOST], left, head_weight, n_dev, span, per_dev)
    rest = [own, below, *beside, above][MOST:] + [*corners, *far]
    for at in range(0, len(rest), MOST):
        sent = late(rest[at : at + MOST], (left, right), sent, n_dev, span, per_dev)
    everything = lax.all_to_all(sent, ("tok", "voc"), 0, 0, tiled=True)
    return finish(everything, req_dev, span)


def solution(mesh):
    placed = (
        P(("tok", "voc"), None, None),
        P(),
        P(None, "voc"),
        P(("tok", "voc")),
        P(("tok", "voc")),
        P(),
        P(("tok", "voc"), None),
    )
    return jax.shard_map(
        functools.partial(shards, mesh.shape["tok"], mesh.shape["voc"]),
        mesh=mesh,
        in_specs=placed,
        out_specs=(P(("tok", "voc"), None), P(("tok", "voc"), None)),
        check_vma=False,
    )
```

```python
import functools

import jax
import jax.numpy as jnp
from jax import lax
from jax.experimental import pallas as pl
from jax.experimental.pallas import tpu as pltpu
from jax.sharding import PartitionSpec as P

EPS = 1e-06
LIVE = 24
RING = 4
LANES = 128
DIGIT = 7
TAIL = 16
NOWHERE = (1 << (2 * DIGIT)) - 1
STATS = 4
TILE = 1280
SHORT = 512
MOST = 4
CUT = 2560
PIECE = 1280
F32 = jnp.float32
BF16 = jnp.bfloat16
VMEM = pltpu.VMEM
MIB = 2**20


def iota(shape, dim):
    return lax.broadcasted_iota(jnp.int32, shape, dim)


def pack_kernel(n_voc, *refs):
    sources, out_ref, copies, sems = refs[:6], refs[6], refs[7:13], refs[13]
    started = [pltpu.make_async_copy(a, b, sems.at[at]) for at, (a, b) in enumerate(zip(sources, copies))]
    for copy in started:
        copy.start()
    for copy in started:
        copy.wait()
    offset_ref, length_ref, request_ref, hidden_ref, gain_ref, target_ref = copies
    req_dev, span, width = hidden_ref.shape
    rows = req_dev * LIVE
    device = lax.axis_index("tok") * n_voc + lax.axis_index("voc")
    values = hidden_ref[...].reshape(req_dev * span, width).astype(F32)
    square = jnp.mean(values * values, axis=-1, keepdims=True)
    normed = (values * lax.rsqrt(square + EPS) * gain_ref[...]).astype(BF16)

    def window(row):
        source = place = jnp.zeros(row.shape, jnp.int32) + NOWHERE
        for slot in range(req_dev):
            step = row - slot * LIVE
            mine = (step >= 0) & (step < LIVE)
            position = offset_ref[slot] + step
            request = request_ref[device * req_dev + slot]
            source = jnp.where(mine, slot * span + position, source)
            place = jnp.where(mine & (step < length_ref[slot]), request * span + position, place)
        return source, place

    source, _ = window(iota((rows, 1), 0))
    taken = (iota((rows, req_dev * span), 1) == source).astype(BF16)
    sent = jnp.dot(taken, normed, preferred_element_type=F32).astype(BF16)
    for at in range(width // LANES):
        out_ref[at * rows : (at + 1) * rows, :] = sent[:, at * LANES : (at + 1) * LANES]
    source, place = window(iota((1, LANES), 1))
    taken = (iota((req_dev * span, LANES), 0) == source).astype(BF16)
    target = jnp.concatenate([target_ref[slot : slot + 1, :] for slot in range(req_dev)], axis=1)
    low = (1 << DIGIT) - 1
    kind = iota((TAIL, req_dev * span), 0)
    digits = jnp.zeros((TAIL, req_dev * span), jnp.int32)
    for at, digit in enumerate((target >> (2 * DIGIT), (target >> DIGIT) & low, target & low)):
        digits = jnp.where(kind == at, digit, digits)
    tail = jnp.dot(digits.astype(F32).astype(BF16), taken, preferred_element_type=F32)
    kind = iota((TAIL, LANES), 0)
    for at, digit in enumerate((place >> DIGIT, place & low)):
        tail = jnp.where(kind == at + 3, digit.astype(F32), tail)
    out_ref[width // LANES * rows :, :] = tail.astype(BF16)


def pack(hidden, norm_gain, lengths, offsets, slot_request, targets, n_voc):
    req_dev, _, width = hidden.shape
    arrays = (offsets, lengths, slot_request, hidden, norm_gain.reshape(1, -1), targets)
    spaces = (pltpu.SMEM,) * 3 + (VMEM,) * 3
    return pl.pallas_call(
        functools.partial(pack_kernel, n_voc),
        out_shape=jax.ShapeDtypeStruct((width // LANES * req_dev * LIVE + TAIL, LANES), BF16),
        in_specs=[pl.BlockSpec(memory_space=pl.ANY)] * 6,
        out_specs=pl.BlockSpec(memory_space=VMEM),
        scratch_shapes=[space(a.shape, a.dtype) for space, a in zip(spaces, arrays)]
        + [pltpu.SemaphoreType.DMA((6,))],
        compiler_params=pltpu.CompilerParams(vmem_limit_bytes=8 * MIB),
        name="pack",
    )(*(pltpu.with_memory_space_constraint(a, pltpu.HBM) for a in arrays))


def decode(tail):
    at, column = iota((TAIL, 2 * LANES), 0), iota((TAIL, 2 * LANES), 1)
    scale = jnp.zeros((TAIL, 2 * LANES), F32)
    for row, value in enumerate((1 << (2 * DIGIT), 1 << DIGIT, 1, 1 << DIGIT, 1)):
        scale = jnp.where((at == row) & ((column < LANES) == (row < 3)), float(value), scale)
    both = lax.dot_general(tail, scale.astype(BF16), (((0,), (0,)), ((), ())), preferred_element_type=F32)
    return both[:, :LANES], both[:, LANES:]


def tiles(columns, size):
    return [(base, min(size, columns - base)) for base in range(0, columns, size)]


def shorten(plan):
    *plan, (weight_ref, column, base, wide, copy) = plan
    cut = max(wide - SHORT, 0)
    head = [(weight_ref, column, base, cut, copy)] if cut else []
    return plan + head + [(weight_ref, column + cut, base + cut, wide - cut, None if cut else copy)]


def height(block, width):
    return (block.shape[0] - TAIL) * LANES // width


def assemble(blocks, x_ref, place_ref):
    width = x_ref.shape[1]
    size = height(blocks[0], width)
    targets = []
    for at, block in enumerate(blocks):
        rows = slice(at * size, (at + 1) * size)
        for part in range(width // LANES):
            x_ref[rows, part * LANES : (part + 1) * LANES] = block[part * size : (part + 1) * size, :]
        target, place = decode(block[width // LANES * size :, :])
        place_ref[rows, :] = place[:size]
        targets.append(target[:size])
    return jnp.concatenate(targets, axis=0)


def take(logits_ref, state, wanted, base, wide, fresh):
    peak_ref, sum_ref, dot_ref, pick_ref = state
    peak = functools.reduce(jnp.maximum, [logits_ref[:, at : at + LANES] for at in range(0, wide, LANES)])
    if fresh:
        total = dots = pick = jnp.zeros_like(peak)
    else:
        old = peak_ref[...]
        peak = jnp.maximum(old, peak)
        drop = old - peak
        scale = jnp.exp(drop)
        total = sum_ref[...]
        dots = (dot_ref[...] + drop * total) * scale
        total = total * scale
        pick = pick_ref[...]
    for at in range(0, wide, LANES):
        part = logits_ref[:, at : at + LANES]
        below = part - peak
        weight = jnp.exp(below)
        total += weight
        dots += weight * below
        pick = jnp.where(wanted == float(base + at), part, pick)
    peak_ref[...] = peak
    sum_ref[...] = total
    dot_ref[...] = dots
    pick_ref[...] = pick


def route(state, place_ref, before_ref, out_ref, span, per_dev):
    peak_ref, sum_ref, dot_ref, pick_ref = state
    rows = place_ref.shape[0]
    shift = span.bit_length() - 1
    lane = iota((rows, LANES), 1).astype(F32)
    peak = jnp.max(peak_ref[...], axis=1, keepdims=True)
    drop = peak_ref[...] - peak
    scale = jnp.exp(drop)
    total = jnp.sum(sum_ref[...] * scale, axis=1, keepdims=True)
    dots = jnp.sum((dot_ref[...] + drop * sum_ref[...]) * scale, axis=1, keepdims=True)
    pick = jnp.sum(pick_ref[...], axis=1, keepdims=True)
    stats = jnp.zeros((rows, LANES), F32)
    for at, value in enumerate((peak, total, dots, pick)):
        high = value.astype(BF16).astype(F32)
        middle = (value - high).astype(BF16).astype(F32)
        low = value - high - middle
        for part, piece in enumerate((high, middle, low)):
            stats = jnp.where(lane == float(8 * part + at), piece, stats)
    stats = stats.T.astype(BF16)[:32]
    lane = iota((STATS, LANES), 1)
    slots = []
    for first_row in range(0, rows, LIVE):
        request = jnp.broadcast_to(place_ref[first_row : first_row + 1, :].astype(jnp.int32) >> shift, (STATS, LANES))
        spot = (request * span + (lane & (span - 1))).astype(F32)[:1]
        there = (place_ref[...] == spot).astype(F32).astype(BF16)
        moved = jnp.dot(stats, there, preferred_element_type=F32)
        slots.append((request, (moved[0:8] + moved[8:16] + moved[16:24])[:STATS]))
    for group in range(out_ref.shape[0] * per_dev // LANES):
        held = group * (LANES // span) + (lane >> shift)
        total = jnp.zeros((STATS, LANES), F32)
        for request, moved in slots:
            total = jnp.where(request == held, moved, total)
        for at in range(LANES // per_dev):
            to = group * (LANES // per_dev) + at
            part = total[:, at * per_dev : (at + 1) * per_dev]
            if before_ref is not None:
                part += before_ref[to, :, :per_dev]
            out_ref[to, :, :per_dev] = part


def sweep(x_ref, plan, logits, state, wanted):
    last = None
    for at, (weight_ref, column, base, wide, copy) in enumerate(plan):
        if copy is not None:
            copy.wait()
        logits[at % 2][:, :wide] = jnp.dot(
            x_ref[...], weight_ref[:, column : column + wide], preferred_element_type=F32
        )
        if last is not None:
            take(*last)
        last = logits[at % 2], state, wanted, base, wide, at == 0
    take(*last)


def wanted_columns(target, vocab_dev):
    first = (lax.axis_index("voc") * vocab_dev).astype(F32)
    return target - first - iota(target.shape, 1).astype(F32)


def fetch(weight_ref, held_ref, sems, lo):
    started = []
    for at, (base, wide) in enumerate(tiles(held_ref.shape[1], PIECE)):
        copy = pltpu.make_async_copy(
            weight_ref.at[:, pl.ds(lo + base, wide)], held_ref.at[:, pl.ds(base, wide)], sems.at[at]
        )
        copy.start()
        started.append((base, wide, copy))
    return started


def preload_kernel(after_ref, weight_ref, held_ref, sems):
    for _, _, copy in fetch(weight_ref, held_ref, sems, 0):
        copy.wait()


def early_kernel(count, span, per_dev, *refs):
    blocks, (first_ref, weight_ref, *refs) = refs[:count], refs[count:]
    out_ref, held_ref, x_ref, place_ref, even_ref, odd_ref, sems, *state = refs
    cut = first_ref.shape[1]
    copies = fetch(weight_ref, held_ref, sems, cut)
    target = assemble(blocks, x_ref, place_ref)
    plan = [(first_ref, base, base, wide, None) for base, wide in tiles(cut, TILE)]
    plan += [(held_ref, base, cut + base, wide, copy) for base, wide, copy in copies]
    sweep(x_ref, shorten(plan), (even_ref, odd_ref), state, wanted_columns(target, weight_ref.shape[1]))
    route(state, place_ref, None, out_ref, span, per_dev)


def late_kernel(count, span, per_dev, *refs):
    blocks, (first_ref, second_ref, before_ref, *refs) = refs[:count], refs[count:]
    out_ref, x_ref, place_ref, even_ref, odd_ref, *state = refs
    cut = first_ref.shape[1]
    target = assemble(blocks, x_ref, place_ref)
    plan = [(first_ref, base, base, wide, None) for base, wide in tiles(cut, TILE)]
    plan += [(second_ref, base, cut + base, wide, None) for base, wide in tiles(second_ref.shape[1], TILE)]
    sweep(x_ref, shorten(plan), (even_ref, odd_ref), state, wanted_columns(target, cut + second_ref.shape[1]))
    route(state, place_ref, before_ref, out_ref, span, per_dev)


def call(kernel, name, operands, spaces, out_shape, rows, width, scratch, columns):
    specs = [pl.BlockSpec(memory_space=pl.ANY if space is pltpu.HBM else VMEM) for space in spaces]
    operands = [
        a if space is None else pltpu.with_memory_space_constraint(a, space) for a, space in zip(operands, spaces)
    ]
    return pl.pallas_call(
        kernel,
        out_shape=out_shape,
        in_specs=specs,
        out_specs=jax.tree.map(lambda _: pl.BlockSpec(memory_space=VMEM), out_shape),
        scratch_shapes=[VMEM((rows, width), BF16), VMEM((rows, LANES), F32)] + [VMEM((rows, TILE), F32)] * 2 + scratch,
        compiler_params=pltpu.CompilerParams(vmem_limit_bytes=10 * MIB),
        cost_estimate=pl.CostEstimate(
            flops=2 * rows * width * columns, bytes_accessed=2 * width * columns, transcendentals=rows * columns
        ),
        name=name,
    )(*operands)


def preload(after, weight, cut):
    return pl.pallas_call(
        preload_kernel,
        out_shape=VMEM((weight.shape[0], cut), BF16),
        in_specs=[pl.BlockSpec(memory_space=pl.ANY)] * 2,
        out_specs=pl.BlockSpec(memory_space=VMEM),
        scratch_shapes=[pltpu.SemaphoreType.DMA((len(tiles(cut, PIECE)),))],
        compiler_params=pltpu.CompilerParams(vmem_limit_bytes=MIB),
        name="preload",
    )(after, pltpu.with_memory_space_constraint(weight, pltpu.HBM))


def early(blocks, first, weight, n_dev, span, per_dev):
    width = weight.shape[0]
    rows = len(blocks) * height(blocks[0], width)
    rest = weight.shape[1] - first.shape[1]
    return call(
        functools.partial(early_kernel, len(blocks), span, per_dev),
        "early",
        (*blocks, first, weight),
        (VMEM,) * (len(blocks) + 1) + (pltpu.HBM,),
        (jax.ShapeDtypeStruct((n_dev, STATS, LANES), F32), VMEM((width, rest), BF16)),
        rows,
        width,
        [pltpu.SemaphoreType.DMA((len(tiles(rest, PIECE)),))] + [VMEM((rows, LANES), F32)] * STATS,
        weight.shape[1],
    )


def late(blocks, held, before, n_dev, span, per_dev):
    width = held[0].shape[0]
    rows = len(blocks) * height(blocks[0], width)
    return call(
        functools.partial(late_kernel, len(blocks), span, per_dev),
        "late",
        (*blocks, *held, before),
        (VMEM,) * (len(blocks) + 2) + (None,),
        jax.ShapeDtypeStruct((n_dev, STATS, LANES), F32),
        rows,
        width,
        [VMEM((rows, LANES), F32)] * STATS,
        sum(a.shape[1] for a in held),
    )


def finish_kernel(all_ref, logprob_ref, entropy_ref):
    req_dev, span = logprob_ref.shape
    peak, total, dots, pick = (all_ref[:, at, :] for at in range(4))
    held = total > 0.0
    top = jnp.max(jnp.where(held, peak, -jnp.inf), axis=0, keepdims=True)
    scored = top > -jnp.inf
    top = jnp.where(scored, top, 0.0)
    drop = jnp.where(held, peak - top, 0.0)
    scale = jnp.exp(drop)
    whole = jnp.sum(total * scale, axis=0, keepdims=True)
    whole = jnp.where(scored, whole, 1.0)
    mean = jnp.sum((dots + drop * total) * scale, axis=0, keepdims=True) / whole
    log_total = jnp.log(whole)
    logprob = jnp.where(scored, jnp.sum(pick, axis=0, keepdims=True) - top - log_total, 0.0)
    entropy = jnp.where(scored, log_total - mean, 0.0)
    for at in range(req_dev):
        logprob_ref[at : at + 1, :] = logprob[:, at * span : (at + 1) * span]
        entropy_ref[at : at + 1, :] = entropy[:, at * span : (at + 1) * span]


def finish(everything, req_dev, span):
    vmem = pl.BlockSpec(memory_space=VMEM)
    shape = jax.ShapeDtypeStruct((req_dev, span), F32)
    return pl.pallas_call(
        finish_kernel,
        out_shape=(shape, shape),
        in_specs=[vmem],
        out_specs=(vmem, vmem),
        compiler_params=pltpu.CompilerParams(vmem_limit_bytes=8 * MIB),
        name="finish",
    )(everything)


def shift(block, along_z, along_y, n_voc):
    side = n_voc // RING
    pairs = [
        (z * side + y, (z + along_z) % RING * side + (y + along_y) % side)
        for z in range(RING)
        for y in range(side)
    ]
    return lax.ppermute(block, "voc", pairs)


def shards(n_tok, n_voc, hidden, norm_gain, head_weight, lengths, offsets, slot_request, targets):
    req_dev, span, _ = hidden.shape
    n_dev, per_dev = n_tok * n_voc, req_dev * span
    over_y = range(1, n_voc // RING)
    own = pack(hidden, norm_gain, lengths, offsets, slot_request, targets, n_voc)
    below = shift(own, 1, 0, n_voc)
    beside = [shift(own, 0, y, n_voc) for y in over_y]
    above = shift(own, -1, 0, n_voc)
    left = preload(own, head_weight, CUT)
    left, below, beside = lax.optimization_barrier((left, below, beside))
    far = [shift(below, 1, y, n_voc) for y in range(n_voc // RING)]
    corners = [shift(a, 0, y, n_voc) for y in over_y for a in (below, above)]
    sent, right = early([own, below, *beside, above][:MOST], left, head_weight, n_dev, span, per_dev)
    rest = [own, below, *beside, above][MOST:] + [*corners, *far]
    for at in range(0, len(rest), MOST):
        sent = late(rest[at : at + MOST], (left, right), sent, n_dev, span, per_dev)
    everything = lax.all_to_all(sent, ("tok", "voc"), 0, 0, tiled=True)
    return finish(everything, req_dev, span)


def solution(mesh):
    placed = (
        P(("tok", "voc"), None, None),
        P(),
        P(None, "voc"),
        P(("tok", "voc")),
        P(("tok", "voc")),
        P(),
        P(("tok", "voc"), None),
    )
    return jax.shard_map(
        functools.partial(shards, mesh.shape["tok"], mesh.shape["voc"]),
        mesh=mesh,
        in_specs=placed,
        out_specs=(P(("tok", "voc"), None), P(("tok", "voc"), None)),
        check_vma=False,
    )
```

```python
import functools

import jax
import jax.numpy as jnp
from jax import lax
from jax.experimental import pallas as pl
from jax.experimental.pallas import tpu as pltpu
from jax.sharding import PartitionSpec as P

EPS = 1e-06
LIVE = 24
RING = 4
LANES = 128
DIGIT = 7
TAIL = 16
NOWHERE = (1 << (2 * DIGIT)) - 1
STATS = 4
TILE = 1280
SHORT = 256
MOST = 4
CUT = 2560
PIECE = 1280
F32 = jnp.float32
BF16 = jnp.bfloat16
VMEM = pltpu.VMEM
MIB = 2**20


def iota(shape, dim):
    return lax.broadcasted_iota(jnp.int32, shape, dim)


def pack_kernel(n_voc, *refs):
    sources, out_ref, copies, sems = refs[:6], refs[6], refs[7:13], refs[13]
    started = [pltpu.make_async_copy(a, b, sems.at[at]) for at, (a, b) in enumerate(zip(sources, copies))]
    for copy in started:
        copy.start()
    for copy in started:
        copy.wait()
    offset_ref, length_ref, request_ref, hidden_ref, gain_ref, target_ref = copies
    req_dev, span, width = hidden_ref.shape
    rows = req_dev * LIVE
    device = lax.axis_index("tok") * n_voc + lax.axis_index("voc")
    values = hidden_ref[...].reshape(req_dev * span, width).astype(F32)
    square = jnp.mean(values * values, axis=-1, keepdims=True)
    normed = (values * lax.rsqrt(square + EPS) * gain_ref[...]).astype(BF16)

    def window(row):
        source = place = jnp.zeros(row.shape, jnp.int32) + NOWHERE
        for slot in range(req_dev):
            step = row - slot * LIVE
            mine = (step >= 0) & (step < LIVE)
            position = offset_ref[slot] + step
            request = request_ref[device * req_dev + slot]
            source = jnp.where(mine, slot * span + position, source)
            place = jnp.where(mine & (step < length_ref[slot]), request * span + position, place)
        return source, place

    source, _ = window(iota((rows, 1), 0))
    taken = (iota((rows, req_dev * span), 1) == source).astype(BF16)
    sent = jnp.dot(taken, normed, preferred_element_type=F32).astype(BF16)
    for at in range(width // LANES):
        out_ref[at * rows : (at + 1) * rows, :] = sent[:, at * LANES : (at + 1) * LANES]
    source, place = window(iota((1, LANES), 1))
    taken = (iota((req_dev * span, LANES), 0) == source).astype(BF16)
    target = jnp.concatenate([target_ref[slot : slot + 1, :] for slot in range(req_dev)], axis=1)
    low = (1 << DIGIT) - 1
    kind = iota((TAIL, req_dev * span), 0)
    digits = jnp.zeros((TAIL, req_dev * span), jnp.int32)
    for at, digit in enumerate((target >> (2 * DIGIT), (target >> DIGIT) & low, target & low)):
        digits = jnp.where(kind == at, digit, digits)
    tail = jnp.dot(digits.astype(F32).astype(BF16), taken, preferred_element_type=F32)
    kind = iota((TAIL, LANES), 0)
    for at, digit in enumerate((place >> DIGIT, place & low)):
        tail = jnp.where(kind == at + 3, digit.astype(F32), tail)
    out_ref[width // LANES * rows :, :] = tail.astype(BF16)


def pack(hidden, norm_gain, lengths, offsets, slot_request, targets, n_voc):
    req_dev, _, width = hidden.shape
    arrays = (offsets, lengths, slot_request, hidden, norm_gain.reshape(1, -1), targets)
    spaces = (pltpu.SMEM,) * 3 + (VMEM,) * 3
    return pl.pallas_call(
        functools.partial(pack_kernel, n_voc),
        out_shape=jax.ShapeDtypeStruct((width // LANES * req_dev * LIVE + TAIL, LANES), BF16),
        in_specs=[pl.BlockSpec(memory_space=pl.ANY)] * 6,
        out_specs=pl.BlockSpec(memory_space=VMEM),
        scratch_shapes=[space(a.shape, a.dtype) for space, a in zip(spaces, arrays)]
        + [pltpu.SemaphoreType.DMA((6,))],
        compiler_params=pltpu.CompilerParams(vmem_limit_bytes=8 * MIB),
        name="pack",
    )(*(pltpu.with_memory_space_constraint(a, pltpu.HBM) for a in arrays))


def decode(tail):
    at, column = iota((TAIL, 2 * LANES), 0), iota((TAIL, 2 * LANES), 1)
    scale = jnp.zeros((TAIL, 2 * LANES), F32)
    for row, value in enumerate((1 << (2 * DIGIT), 1 << DIGIT, 1, 1 << DIGIT, 1)):
        scale = jnp.where((at == row) & ((column < LANES) == (row < 3)), float(value), scale)
    both = lax.dot_general(tail, scale.astype(BF16), (((0,), (0,)), ((), ())), preferred_element_type=F32)
    return both[:, :LANES], both[:, LANES:]


def tiles(columns, size):
    return [(base, min(size, columns - base)) for base in range(0, columns, size)]


def shorten(plan):
    *plan, (weight_ref, column, base, wide, copy) = plan
    cut = max(wide - SHORT, 0)
    head = [(weight_ref, column, base, cut, copy)] if cut else []
    return plan + head + [(weight_ref, column + cut, base + cut, wide - cut, None if cut else copy)]


def height(block, width):
    return (block.shape[0] - TAIL) * LANES // width


def assemble(blocks, x_ref, place_ref):
    width = x_ref.shape[1]
    size = height(blocks[0], width)
    targets = []
    for at, block in enumerate(blocks):
        rows = slice(at * size, (at + 1) * size)
        for part in range(width // LANES):
            x_ref[rows, part * LANES : (part + 1) * LANES] = block[part * size : (part + 1) * size, :]
        target, place = decode(block[width // LANES * size :, :])
        place_ref[rows, :] = place[:size]
        targets.append(target[:size])
    return jnp.concatenate(targets, axis=0)


def take(logits_ref, state, wanted, base, wide, fresh):
    peak_ref, sum_ref, dot_ref, pick_ref = state
    peak = functools.reduce(jnp.maximum, [logits_ref[:, at : at + LANES] for at in range(0, wide, LANES)])
    if fresh:
        total = dots = pick = jnp.zeros_like(peak)
    else:
        old = peak_ref[...]
        peak = jnp.maximum(old, peak)
        drop = old - peak
        scale = jnp.exp(drop)
        total = sum_ref[...]
        dots = (dot_ref[...] + drop * total) * scale
        total = total * scale
        pick = pick_ref[...]
    for at in range(0, wide, LANES):
        part = logits_ref[:, at : at + LANES]
        below = part - peak
        weight = jnp.exp(below)
        total += weight
        dots += weight * below
        pick = jnp.where(wanted == float(base + at), part, pick)
    peak_ref[...] = peak
    sum_ref[...] = total
    dot_ref[...] = dots
    pick_ref[...] = pick


def route(state, place_ref, before_ref, out_ref, span, per_dev):
    peak_ref, sum_ref, dot_ref, pick_ref = state
    rows = place_ref.shape[0]
    shift = span.bit_length() - 1
    lane = iota((rows, LANES), 1).astype(F32)
    peak = jnp.max(peak_ref[...], axis=1, keepdims=True)
    drop = peak_ref[...] - peak
    scale = jnp.exp(drop)
    total = jnp.sum(sum_ref[...] * scale, axis=1, keepdims=True)
    dots = jnp.sum((dot_ref[...] + drop * sum_ref[...]) * scale, axis=1, keepdims=True)
    pick = jnp.sum(pick_ref[...], axis=1, keepdims=True)
    stats = jnp.zeros((rows, LANES), F32)
    for at, value in enumerate((peak, total, dots, pick)):
        high = value.astype(BF16).astype(F32)
        middle = (value - high).astype(BF16).astype(F32)
        low = value - high - middle
        for part, piece in enumerate((high, middle, low)):
            stats = jnp.where(lane == float(8 * part + at), piece, stats)
    stats = stats.T.astype(BF16)[:32]
    lane = iota((STATS, LANES), 1)
    slots = []
    for first_row in range(0, rows, LIVE):
        request = jnp.broadcast_to(place_ref[first_row : first_row + 1, :].astype(jnp.int32) >> shift, (STATS, LANES))
        spot = (request * span + (lane & (span - 1))).astype(F32)[:1]
        there = (place_ref[...] == spot).astype(F32).astype(BF16)
        moved = jnp.dot(stats, there, preferred_element_type=F32)
        slots.append((request, (moved[0:8] + moved[8:16] + moved[16:24])[:STATS]))
    for group in range(out_ref.shape[0] * per_dev // LANES):
        held = group * (LANES // span) + (lane >> shift)
        total = jnp.zeros((STATS, LANES), F32)
        for request, moved in slots:
            total = jnp.where(request == held, moved, total)
        for at in range(LANES // per_dev):
            to = group * (LANES // per_dev) + at
            part = total[:, at * per_dev : (at + 1) * per_dev]
            if before_ref is not None:
                part += before_ref[to, :, :per_dev]
            out_ref[to, :, :per_dev] = part


def sweep(x_ref, plan, logits, state, wanted):
    last = None
    for at, (weight_ref, column, base, wide, copy) in enumerate(plan):
        if copy is not None:
            copy.wait()
        logits[at % 2][:, :wide] = jnp.dot(
            x_ref[...], weight_ref[:, column : column + wide], preferred_element_type=F32
        )
        if last is not None:
            take(*last)
        last = logits[at % 2], state, wanted, base, wide, at == 0
    take(*last)


def wanted_columns(target, vocab_dev):
    first = (lax.axis_index("voc") * vocab_dev).astype(F32)
    return target - first - iota(target.shape, 1).astype(F32)


def fetch(weight_ref, held_ref, sems, lo):
    started = []
    for at, (base, wide) in enumerate(tiles(held_ref.shape[1], PIECE)):
        copy = pltpu.make_async_copy(
            weight_ref.at[:, pl.ds(lo + base, wide)], held_ref.at[:, pl.ds(base, wide)], sems.at[at]
        )
        copy.start()
        started.append((base, wide, copy))
    return started


def preload_kernel(after_ref, weight_ref, held_ref, sems):
    for _, _, copy in fetch(weight_ref, held_ref, sems, 0):
        copy.wait()


def early_kernel(count, span, per_dev, *refs):
    blocks, (first_ref, weight_ref, *refs) = refs[:count], refs[count:]
    out_ref, held_ref, x_ref, place_ref, even_ref, odd_ref, sems, *state = refs
    cut = first_ref.shape[1]
    copies = fetch(weight_ref, held_ref, sems, cut)
    target = assemble(blocks, x_ref, place_ref)
    plan = [(first_ref, base, base, wide, None) for base, wide in tiles(cut, TILE)]
    plan += [(held_ref, base, cut + base, wide, copy) for base, wide, copy in copies]
    sweep(x_ref, shorten(plan), (even_ref, odd_ref), state, wanted_columns(target, weight_ref.shape[1]))
    route(state, place_ref, None, out_ref, span, per_dev)


def late_kernel(count, span, per_dev, *refs):
    blocks, (first_ref, second_ref, before_ref, *refs) = refs[:count], refs[count:]
    out_ref, x_ref, place_ref, even_ref, odd_ref, *state = refs
    cut = first_ref.shape[1]
    target = assemble(blocks, x_ref, place_ref)
    plan = [(first_ref, base, base, wide, None) for base, wide in tiles(cut, TILE)]
    plan += [(second_ref, base, cut + base, wide, None) for base, wide in tiles(second_ref.shape[1], TILE)]
    sweep(x_ref, shorten(plan), (even_ref, odd_ref), state, wanted_columns(target, cut + second_ref.shape[1]))
    route(state, place_ref, before_ref, out_ref, span, per_dev)


def call(kernel, name, operands, spaces, out_shape, rows, width, scratch, columns):
    specs = [pl.BlockSpec(memory_space=pl.ANY if space is pltpu.HBM else VMEM) for space in spaces]
    operands = [
        a if space is None else pltpu.with_memory_space_constraint(a, space) for a, space in zip(operands, spaces)
    ]
    return pl.pallas_call(
        kernel,
        out_shape=out_shape,
        in_specs=specs,
        out_specs=jax.tree.map(lambda _: pl.BlockSpec(memory_space=VMEM), out_shape),
        scratch_shapes=[VMEM((rows, width), BF16), VMEM((rows, LANES), F32)] + [VMEM((rows, TILE), F32)] * 2 + scratch,
        compiler_params=pltpu.CompilerParams(vmem_limit_bytes=10 * MIB),
        cost_estimate=pl.CostEstimate(
            flops=2 * rows * width * columns, bytes_accessed=2 * width * columns, transcendentals=rows * columns
        ),
        name=name,
    )(*operands)


def preload(after, weight, cut):
    return pl.pallas_call(
        preload_kernel,
        out_shape=VMEM((weight.shape[0], cut), BF16),
        in_specs=[pl.BlockSpec(memory_space=pl.ANY)] * 2,
        out_specs=pl.BlockSpec(memory_space=VMEM),
        scratch_shapes=[pltpu.SemaphoreType.DMA((len(tiles(cut, PIECE)),))],
        compiler_params=pltpu.CompilerParams(vmem_limit_bytes=MIB),
        name="preload",
    )(after, pltpu.with_memory_space_constraint(weight, pltpu.HBM))


def early(blocks, first, weight, n_dev, span, per_dev):
    width = weight.shape[0]
    rows = len(blocks) * height(blocks[0], width)
    rest = weight.shape[1] - first.shape[1]
    return call(
        functools.partial(early_kernel, len(blocks), span, per_dev),
        "early",
        (*blocks, first, weight),
        (VMEM,) * (len(blocks) + 1) + (pltpu.HBM,),
        (jax.ShapeDtypeStruct((n_dev, STATS, LANES), F32), VMEM((width, rest), BF16)),
        rows,
        width,
        [pltpu.SemaphoreType.DMA((len(tiles(rest, PIECE)),))] + [VMEM((rows, LANES), F32)] * STATS,
        weight.shape[1],
    )


def late(blocks, held, before, n_dev, span, per_dev):
    width = held[0].shape[0]
    rows = len(blocks) * height(blocks[0], width)
    return call(
        functools.partial(late_kernel, len(blocks), span, per_dev),
        "late",
        (*blocks, *held, before),
        (VMEM,) * (len(blocks) + 2) + (None,),
        jax.ShapeDtypeStruct((n_dev, STATS, LANES), F32),
        rows,
        width,
        [VMEM((rows, LANES), F32)] * STATS,
        sum(a.shape[1] for a in held),
    )


def finish_kernel(all_ref, logprob_ref, entropy_ref):
    req_dev, span = logprob_ref.shape
    peak, total, dots, pick = (all_ref[:, at, :] for at in range(4))
    held = total > 0.0
    top = jnp.max(jnp.where(held, peak, -jnp.inf), axis=0, keepdims=True)
    scored = top > -jnp.inf
    top = jnp.where(scored, top, 0.0)
    drop = jnp.where(held, peak - top, 0.0)
    scale = jnp.exp(drop)
    whole = jnp.sum(total * scale, axis=0, keepdims=True)
    whole = jnp.where(scored, whole, 1.0)
    mean = jnp.sum((dots + drop * total) * scale, axis=0, keepdims=True) / whole
    log_total = jnp.log(whole)
    logprob = jnp.where(scored, jnp.sum(pick, axis=0, keepdims=True) - top - log_total, 0.0)
    entropy = jnp.where(scored, log_total - mean, 0.0)
    for at in range(req_dev):
        logprob_ref[at : at + 1, :] = logprob[:, at * span : (at + 1) * span]
        entropy_ref[at : at + 1, :] = entropy[:, at * span : (at + 1) * span]


def finish(everything, req_dev, span):
    vmem = pl.BlockSpec(memory_space=VMEM)
    shape = jax.ShapeDtypeStruct((req_dev, span), F32)
    return pl.pallas_call(
        finish_kernel,
        out_shape=(shape, shape),
        in_specs=[vmem],
        out_specs=(vmem, vmem),
        compiler_params=pltpu.CompilerParams(vmem_limit_bytes=8 * MIB),
        name="finish",
    )(everything)


def shift(block, along_z, along_y, n_voc):
    side = n_voc // RING
    pairs = [
        (z * side + y, (z + along_z) % RING * side + (y + along_y) % side)
        for z in range(RING)
        for y in range(side)
    ]
    return lax.ppermute(block, "voc", pairs)


def shards(n_tok, n_voc, hidden, norm_gain, head_weight, lengths, offsets, slot_request, targets):
    req_dev, span, _ = hidden.shape
    n_dev, per_dev = n_tok * n_voc, req_dev * span
    over_y = range(1, n_voc // RING)
    own = pack(hidden, norm_gain, lengths, offsets, slot_request, targets, n_voc)
    below = shift(own, -1, 0, n_voc)
    beside = [shift(own, 0, y, n_voc) for y in over_y]
    above = shift(own, 1, 0, n_voc)
    left = preload(own, head_weight, CUT)
    left, below = lax.optimization_barrier((left, below))
    far = [shift(below, -1, y, n_voc) for y in range(n_voc // RING)]
    corners = [shift(a, 0, y, n_voc) for y in over_y for a in (below, above)]
    sent, right = early([own, below, *beside, above][:MOST], left, head_weight, n_dev, span, per_dev)
    rest = [own, below, *beside, above][MOST:] + [*corners, *far]
    for at in range(0, len(rest), MOST):
        sent = late(rest[at : at + MOST], (left, right), sent, n_dev, span, per_dev)
    everything = lax.all_to_all(sent, ("tok", "voc"), 0, 0, tiled=True)
    return finish(everything, req_dev, span)


def solution(mesh):
    placed = (
        P(("tok", "voc"), None, None),
        P(),
        P(None, "voc"),
        P(("tok", "voc")),
        P(("tok", "voc")),
        P(),
        P(("tok", "voc"), None),
    )
    return jax.shard_map(
        functools.partial(shards, mesh.shape["tok"], mesh.shape["voc"]),
        mesh=mesh,
        in_specs=placed,
        out_specs=(P(("tok", "voc"), None), P(("tok", "voc"), None)),
        check_vma=False,
    )
```
